512 devices in a mesh: dp: 8 (over y_lo, core), row: 8 (over y_hi, x), col: 8 (over z).
Axes of the slice: x: 4, y: 8 (y_hi: 2, y_lo: 4; y = y_hi * 4 + y_lo), z: 8, core: 2. Of those that a mesh axis runs over, the one named last changes fastest.
Arguments:
- tokens: bfloat16 [1024, 9216], P('dp', 'row'), may hold values from -6 to 6
- weight_in: bfloat16 [9216, 24576], P('row', ('dp', 'col')), may hold values from -0.0625 to 0.0625
- weight_out: bfloat16 [24576, 9216], P(('dp', 'col'), 'row'), may hold values from -0.0390625 to 0.0390625
- grad_out: bfloat16 [1024, 9216], P('dp', 'row'), may hold values from -1.5 to 1.5
Outputs:
- layer_out: bfloat16 [1024, 9216], P(('dp', 'col'), 'row')
- grad_tokens: bfloat16 [1024, 9216], P(('dp', 'col'), 'row')
- grad_weight_in: bfloat16 [9216, 24576], P('row', ('dp', 'col'))
- grad_weight_out: bfloat16 [24576, 9216], P(('dp', 'col'), 'row')
The draws below stay inside these ranges and needn't reach their ends.
All inputs are finite; a program needn't handle non-finite values.
Results may differ from the reference program's by a relative error of at most 0.025.
Values may be sent and summed in bfloat16 or wider, within the bound.
A program may use at most 64 MiB of HBM per device.

```python
import jax
import jax.numpy as jnp
from jax import lax

D = 9216
FF = 24576
TOKENS = 1024
N_ROW = 8


def block_scale(key, dims, split, least, high):
    gain, own = 1.0, jax.random.fold_in(key, 6)
    for dim, shards_of in split:
        steps = jnp.exp(jax.random.uniform(jax.random.fold_in(own, dim), (shards_of,), jnp.float32, least / len(split), high / len(split)))
        gain = gain * jnp.repeat(steps, dims[dim] // shards_of).reshape([-1 if axis == dim else 1 for axis in range(len(dims))])
    return gain


def centred(own_key, extent, scale, reach, cuts=(), held_as=jnp.bfloat16):
    entries = jax.random.normal(own_key, extent, jnp.float32) * scale
    if len(cuts) > 0:
        entries = block_scale(own_key, extent, cuts, -0.22, 0.18) * entries
    return jnp.clip(entries, min=-reach, max=reach).astype(held_as)


def setup_inputs(seed: int = 0) -> dict:
    splits = jax.random.split(jax.random.key(seed), 5)
    return {
        "tokens": centred(splits[0], (TOKENS, D), 1.0, 6.0, ((0, 8), (1, 8))),
        "weight_in": centred(splits[1], (D, FF), D ** -0.5, 0.0625, ((0, 8), (1, 64))),
        "weight_out": centred(splits[2], (FF, D), FF ** -0.5, 0.0390625, ((0, 64), (1, 8))),
        "grad_out": centred(splits[3], (TOKENS, D), 0.25, 1.5, ((0, 8), (1, 8))),
    }


def gelu_value(pre_value):
    inner_arg = 0.7978845608 * (pre_value + 0.044715 * pre_value * pre_value * pre_value)
    return 0.5 * pre_value * (1.0 + jnp.tanh(inner_arg))


def gelu_slope(pre_value):
    tanh_part = jnp.tanh(0.7978845608 * (pre_value + 0.044715 * pre_value * pre_value * pre_value))
    inner_slope = 0.7978845608 * (1.0 + 0.134145 * pre_value * pre_value)
    return 0.5 * (1.0 + tanh_part) + 0.5 * pre_value * (1.0 - tanh_part * tanh_part) * inner_slope


def blocked_sum(left, right_rows):
    width = left.shape[1] // N_ROW
    total = jnp.zeros((left.shape[0], right_rows.shape[1]), jnp.float32)
    for block in range(N_ROW):
        part = jnp.dot(left[:, block * width:(block + 1) * width], right_rows[block * width:(block + 1) * width, :], preferred_element_type=jnp.float32)
        rounded = lax.optimization_barrier(part.astype(jnp.bfloat16))
        total = total + rounded.astype(jnp.float32)
    return total


def reference(tokens, weight_in, weight_out, grad_out):
    pre_act = blocked_sum(tokens, weight_in)
    hidden = gelu_value(pre_act).astype(jnp.bfloat16)
    layer_out = jnp.dot(hidden, weight_out, preferred_element_type=jnp.float32).astype(jnp.bfloat16)
    grad_pre = blocked_sum(grad_out, weight_out.T)
    grad_act = (grad_pre * gelu_slope(pre_act)).astype(jnp.bfloat16)
    grad_tokens = jnp.dot(grad_act, weight_in.T, preferred_element_type=jnp.float32).astype(jnp.bfloat16)
    grad_weight_in = jnp.dot(tokens.T, grad_act, preferred_element_type=jnp.float32).astype(jnp.bfloat16)
    grad_weight_out = jnp.dot(hidden.T, grad_out, preferred_element_type=jnp.float32).astype(jnp.bfloat16)
    return (layer_out, grad_tokens, grad_weight_in, grad_weight_out)
```

```python
import functools

import jax
import jax.numpy as jnp
from jax import lax
from jax.experimental import pallas as pl
from jax.experimental.pallas import tpu as pltpu
from jax.sharding import PartitionSpec as P

MESH = pl.DeviceIdType.MESH
BF16 = jnp.bfloat16
F32 = jnp.float32

PLACE = {0: 0, 1: 1, 7: 2, 2: 3, 6: 4, 3: 5, 5: 6, 4: 7}
GROUPS = ((0, 1), (1, 2), (3, 2), (5, 2), (7, 1))


def gelu_value(pre_value):
    inner_arg = 0.7978845608 * (pre_value + 0.044715 * pre_value * pre_value * pre_value)
    return 0.5 * pre_value * (1.0 + jnp.tanh(inner_arg))


def gelu_slope(pre_value):
    tanh_part = jnp.tanh(0.7978845608 * (pre_value + 0.044715 * pre_value * pre_value * pre_value))
    inner_slope = 0.7978845608 * (1.0 + 0.134145 * pre_value * pre_value)
    return 0.5 * (1.0 + tanh_part) + 0.5 * pre_value * (1.0 - tanh_part * tanh_part) * inner_slope


def kernel(
    tokens, weight_in, weight_out, grad_out,
    layer_out, grad_tokens, grad_weight_in, grad_weight_out,
    TK, X, WI, WO, PS, PR, YS, YR, HC, SS, SR, OP, ZS, ZRR, ZRL, FS, FR, FO, OB, GI, GO,
    local_sem, a_send, a_recv, j_send, j_recv, c_send, c_recv, r_send, r_recv, l_send, l_recv,
    p_send, p_recv, y_send, y_recv, h_send, h_recv, s_send, s_recv,
    zr_send, zr_recv, zl_send, zl_recv, f_send, f_recv,
):
    dp = lax.axis_index("dp")
    row = lax.axis_index("row")
    z = lax.axis_index("col")
    y, core = dp // 2, dp % 2
    half, x = row // 4, row % 4

    def device(dp=dp, row=row, col=z):
        return {"dp": dp, "row": row, "col": col}

    sibling = device(dp=y * 2 + (1 - core))
    right, left = device(col=(z + 1) % 8), device(col=(z + 7) % 8)
    across = device(row=(1 - half) * 4 + x)
    y_peers = {j: device(dp=((y + j) % 4) * 2 + core) for j in (1, 2, 3)}
    x_of = {m: (x + m) % 4 for m in (1, 2, 3)}
    x_peers = {m: device(row=half * 4 + x_of[m]) for m in (1, 2, 3)}

    pending = []

    def send(src, dst, ssem, rsem, to):
        copy = pltpu.make_async_remote_copy(
            src_ref=src, dst_ref=dst, send_sem=ssem, recv_sem=rsem, device_id=to, device_id_type=MESH
        )
        copy.start()
        pending.append(copy)

    def arrived(dst, ssem, rsem):
        pltpu.make_async_remote_copy(
            src_ref=dst, dst_ref=dst, send_sem=ssem, recv_sem=rsem, device_id=sibling, device_id_type=MESH
        ).wait_recv()

    fetch = [
        pltpu.make_async_copy(tokens, TK.at[0], local_sem.at[0]),
        pltpu.make_async_copy(grad_out, TK.at[1], local_sem.at[1]),
        pltpu.make_async_copy(weight_in, WI, local_sem.at[2]),
        pltpu.make_async_copy(weight_out, WO, local_sem.at[3]),
    ]
    for copy in fetch:
        copy.start()

    barrier = pltpu.get_barrier_semaphore()
    peers = [sibling, right, left, across, *y_peers.values(), *x_peers.values()]
    for peer in peers:
        pl.semaphore_signal(barrier, inc=1, device_id=peer, device_id_type=MESH)
    pl.semaphore_wait(barrier, len(peers))

    fetch[0].wait()
    fetch[1].wait()
    for j in (1, 2, 3):
        send(TK.at[:, z], X.at[0, :, pl.ds((4 - j) * 16, 16)], a_send.at[j - 1], a_recv.at[3 - j], y_peers[j])
    for r in range(8):
        for a in range(2):
            X[PLACE[r], a, 0:16] = TK[a, (z + r) % 8]
    send(X.at[:, :, 0:16], X.at[:, :, 64:80], j_send, j_recv, sibling)
    fetch[2].wait()
    fetch[3].wait()

    def to_sibling(g):
        q, n = GROUPS[g]
        send(X.at[pl.ds(q, n), :, 16:64], X.at[pl.ds(q, n), :, 80:128], c_send.at[g], c_recv.at[g], sibling)

    def stage_c(g):
        q, n = GROUPS[g]
        if g == 0:
            arrived(X.at[:, :, 64:80], j_send, j_recv)
        arrived(X.at[pl.ds(q, n), :, 80:128], c_send.at[g], c_recv.at[g])
        lhs = X[q:q + n, 0].reshape(n * 128, 1152)
        val = jnp.dot(lhs, WI[...], preferred_element_type=F32).astype(BF16).reshape(n, 4, 32, 384)
        for p in range(4):
            PS[p, q:q + n, 0] = val[:, p]
        lhs = X[q:q + n, 1].reshape(n * 128, 1152)
        val = lax.dot_general(lhs, WO[...], (((1,), (1,)), ((), ())), preferred_element_type=F32)
        val = val.astype(BF16).reshape(n, 4, 32, 384)
        for p in range(4):
            PS[p, q:q + n, 1] = val[:, p]
        for m in (1, 2, 3):
            send(
                PS.at[x_of[m], pl.ds(q, n)], PR.at[m - 1, pl.ds(q, n)],
                p_send.at[g * 3 + m - 1], p_recv.at[g * 3 + m - 1], x_peers[m],
            )

    def stage_d(g):
        q, n = GROUPS[g]
        total = PS[x, q:q + n].astype(F32)
        for m in (1, 2, 3):
            arrived(PR.at[m - 1, pl.ds(q, n)], p_send.at[g * 3 + m - 1], p_recv.at[g * 3 + m - 1])
            total = total + PR[m - 1, q:q + n].astype(F32)
        YS[q:q + n] = total.astype(BF16)
        send(YS.at[pl.ds(q, n)], YR.at[pl.ds(q, n)], y_send.at[g], y_recv.at[g], across)

    def stage_e(g):
        q, n = GROUPS[g]
        arrived(YR.at[pl.ds(q, n)], y_send.at[g], y_recv.at[g])
        pre = YS[q:q + n, 0].astype(F32) + YR[q:q + n, 0].astype(F32)
        grad = YS[q:q + n, 1].astype(F32) + YR[q:q + n, 1].astype(F32)
        HC[q:q + n, 0, x] = gelu_value(pre).astype(BF16)
        HC[q:q + n, 1, x] = (grad * gelu_slope(pre)).astype(BF16)
        for m in (1, 2, 3):
            send(
                HC.at[pl.ds(q, n), :, x], HC.at[pl.ds(q, n), :, x],
                h_send.at[g * 3 + m - 1], h_recv.at[g * 3 + m - 1], x_peers[m],
            )

    def stage_f(g):
        q, n = GROUPS[g]
        for m in (1, 2, 3):
            arrived(HC.at[pl.ds(q, n), :, (x + 4 - m) % 4], h_send.at[g * 3 + m - 1], h_recv.at[g * 3 + m - 1])
        for a in range(2):
            lhs = HC[q:q + n, a].reshape(n * 128, 384)
            if a == 0:
                val = jnp.dot(lhs, WO[...], preferred_element_type=F32)
            else:
                val = lax.dot_general(lhs, WI[...], (((1,), (1,)), ((), ())), preferred_element_type=F32)
            val = val.reshape(n, 2, 64, 1152)
            OP[q:q + n, a] = val[:, 0]
            SS[q:q + n, a] = val[:, 1].astype(BF16)
        send(SS.at[pl.ds(q, n)], SR.at[pl.ds(q, n)], s_send.at[g], s_recv.at[g], sibling)

    def both_cores(r, a):
        return OP[PLACE[r], a] + SR[PLACE[r], a].astype(F32)

    def go_right(r, a):
        send(ZS.at[PLACE[r], a], ZRR.at[r - 1, a], zr_send.at[r * 2 + a], zr_recv.at[r * 2 + a], right)

    def go_left(r, a):
        send(ZS.at[PLACE[r], a], ZRL.at[r - 4, a], zl_send.at[(r - 4) * 2 + a], zl_recv.at[(r - 4) * 2 + a], left)

    def from_left(r, a):
        arrived(ZRR.at[r, a], zr_send.at[(r + 1) * 2 + a], zr_recv.at[(r + 1) * 2 + a])
        return ZRR[r, a].astype(F32)

    def from_right(r, a):
        arrived(ZRL.at[r - 5, a], zl_send.at[(r - 5) * 2 + a], zl_recv.at[(r - 5) * 2 + a])
        return ZRL[r - 5, a].astype(F32)

    def stage_g(g):
        q, n = GROUPS[g]
        arrived(SR.at[pl.ds(q, n)], s_send.at[g], s_recv.at[g])
        if g == 4:
            ZS[PLACE[4], 0] = both_cores(4, 0).astype(BF16)
            go_right(4, 0)
            ZS[PLACE[4], 1] = both_cores(4, 1).astype(BF16)
            go_left(4, 1)
            return
        for a in (0, 1):
            total = both_cores(g, a)
            if g < 3 or a == 0:
                total = total + from_left(g, a)
            ZS[PLACE[g], a] = total.astype(BF16)
            go_right(g, a)
            b = 1 - a
            total = both_cores(8 - g, b)
            if g < 3 or b == 1:
                total = total + from_right(8 - g, b)
            ZS[PLACE[8 - g], b] = total.astype(BF16)
            go_left(8 - g, b)

    def ring(s, a, going_right):
        if going_right:
            send(
                X.at[PLACE[(8 - s) % 8], a, 16:64], X.at[PLACE[7 - s], a, 16:64],
                r_send.at[s * 2 + a], r_recv.at[s * 2 + a], right,
            )
        else:
            send(
                X.at[PLACE[s], a, 16:64], X.at[PLACE[s + 1], a, 16:64],
                l_send.at[s * 2 + a], l_recv.at[s * 2 + a], left,
            )

    def ring_arrived(s, a, going_right):
        if going_right:
            arrived(X.at[PLACE[7 - s], a, 16:64], r_send.at[s * 2 + a], r_recv.at[s * 2 + a])
        else:
            arrived(X.at[PLACE[s + 1], a, 16:64], l_send.at[s * 2 + a], l_recv.at[s * 2 + a])

    for j in (1, 2, 3):
        arrived(X.at[0, :, pl.ds(j * 16, 16)], a_send.at[j - 1], a_recv.at[j - 1])
    for a in (0, 1):
        ring(0, a, True)
        ring(0, 1 - a, False)
    to_sibling(0)
    stage_c(0)
    for s in (1, 2, 3):
        for a in (0, 1):
            ring_arrived(s - 1, a, True)
            if s < 3 or a == 0:
                ring(s, a, True)
            ring_arrived(s - 1, 1 - a, False)
            if s < 3 or a == 0:
                ring(s, 1 - a, False)
        to_sibling(s)
        stage_d(s - 1)
        stage_c(s)
    ring_arrived(3, 0, True)
    ring_arrived(3, 1, False)
    to_sibling(4)
    stage_d(3)
    stage_c(4)
    stage_d(4)
    for g in (3, 4, 2, 1, 0):
        stage_e(g)
    stage_f(4)
    stage_f(3)
    stage_g(4)
    stage_f(2)
    stage_g(3)
    stage_f(1)
    stage_g(2)
    stage_f(0)
    stage_g(1)

    hidden_all, grad_all = HC[:, 0].reshape(1024, 384), HC[:, 1].reshape(1024, 384)

    @pl.loop(0, 9)
    def _(i):
        cols = pl.ds(pl.multiple_of(i * 128, 128), 128)
        lhs = X[:, 0, :, cols].reshape(1024, 128)
        GI[cols, :] = lax.dot_general(
            lhs, grad_all, (((0,), (0,)), ((), ())), preferred_element_type=F32
        ).astype(BF16)
        rhs = X[:, 1, :, cols].reshape(1024, 128)
        GO[:, cols] = lax.dot_general(
            hidden_all, rhs, (((0,), (0,)), ((), ())), preferred_element_type=F32
        ).astype(BF16)

    stores = [
        pltpu.make_async_copy(GI, grad_weight_in, local_sem.at[4]),
        pltpu.make_async_copy(GO, grad_weight_out, local_sem.at[5]),
    ]
    for copy in stores:
        copy.start()

    arrived(SR.at[pl.ds(0, 1)], s_send.at[0], s_recv.at[0])
    for a in (0, 1):
        total = both_cores(0, a) + from_left(0, a) + from_right(8, a)
        FO[a] = total[0:16]
        for j in (1, 2, 3):
            FS[j - 1, a] = total[j * 16:(j + 1) * 16].astype(BF16)
    for j in (1, 2, 3):
        send(FS.at[j - 1], FR.at[j - 1], f_send.at[j - 1], f_recv.at[j - 1], y_peers[j])
    total = FO[...]
    for j in (1, 2, 3):
        arrived(FR.at[j - 1], f_send.at[j - 1], f_recv.at[j - 1])
        total = total + FR[j - 1].astype(F32)
    OB[...] = total.astype(BF16)
    stores.append(pltpu.make_async_copy(OB.at[0], layer_out, local_sem.at[6]))
    stores.append(pltpu.make_async_copy(OB.at[1], grad_tokens, local_sem.at[7]))
    stores[2].start()
    stores[3].start()
    for copy in pending:
        copy.wait_send()
    for copy in stores:
        copy.wait()


def shards(tokens, weight_in, weight_out, grad_out):
    any_space = pl.BlockSpec(memory_space=pl.ANY)
    dma = pltpu.SemaphoreType.DMA
    return pl.pallas_call(
        kernel,
        out_shape=(
            jax.ShapeDtypeStruct((16, 1152), BF16),
            jax.ShapeDtypeStruct((16, 1152), BF16),
            jax.ShapeDtypeStruct((1152, 384), BF16),
            jax.ShapeDtypeStruct((384, 1152), BF16),
        ),
        in_specs=[any_space] * 4,
        out_specs=(any_space,) * 4,
        scratch_shapes=[
            pltpu.VMEM((2, 8, 16, 1152), BF16),
            pltpu.VMEM((8, 2, 128, 1152), BF16),
            pltpu.VMEM((1152, 384), BF16),
            pltpu.VMEM((384, 1152), BF16),
            pltpu.VMEM((4, 8, 2, 32, 384), BF16),
            pltpu.VMEM((3, 8, 2, 32, 384), BF16),
            pltpu.VMEM((8, 2, 32, 384), BF16),
            pltpu.VMEM((8, 2, 32, 384), BF16),
            pltpu.VMEM((8, 2, 4, 32, 384), BF16),
            pltpu.VMEM((8, 2, 64, 1152), BF16),
            pltpu.VMEM((8, 2, 64, 1152), BF16),
            pltpu.VMEM((8, 2, 64, 1152), F32),
            pltpu.VMEM((8, 2, 64, 1152), BF16),
            pltpu.VMEM((4, 2, 64, 1152), BF16),
            pltpu.VMEM((4, 2, 64, 1152), BF16),
            pltpu.VMEM((3, 2, 16, 1152), BF16),
            pltpu.VMEM((3, 2, 16, 1152), BF16),
            pltpu.VMEM((2, 16, 1152), F32),
            pltpu.VMEM((2, 16, 1152), BF16),
            pltpu.VMEM((1152, 384), BF16),
            pltpu.VMEM((384, 1152), BF16),
            dma((8,)),
            dma((3,)), dma((3,)),
            dma, dma,
            dma((5,)), dma((5,)),
            dma((8,)), dma((8,)),
            dma((8,)), dma((8,)),
            dma((15,)), dma((15,)),
            dma((5,)), dma((5,)),
            dma((15,)), dma((15,)),
            dma((5,)), dma((5,)),
            dma((10,)), dma((10,)),
            dma((8,)), dma((8,)),
            dma((3,)), dma((3,)),
        ],
        compiler_params=pltpu.CompilerParams(
            collective_id=0, has_side_effects=True, vmem_limit_bytes=56 * 1024 * 1024
        ),
        cost_estimate=pl.CostEstimate(flops=5436000000, bytes_accessed=8000000, transcendentals=1000000),
    )(tokens.reshape(8, 16, 1152), weight_in, weight_out, grad_out.reshape(8, 16, 1152))


def solution(mesh):
    placed = (P("dp", "row"), P("row", ("dp", "col")), P(("dp", "col"), "row"), P("dp", "row"))
    return jax.shard_map(
        shards,
        mesh=mesh,
        in_specs=placed,
        out_specs=(
            P(("dp", "col"), "row"),
            P(("dp", "col"), "row"),
            P("row", ("dp", "col")),
            P(("dp", "col"), "row"),
        ),
        check_vma=False,
    )
```

```python
import jax
import jax.numpy as jnp
from jax import lax
from jax.experimental import pallas as pl
from jax.experimental.pallas import tpu as pltpu
from jax.sharding import PartitionSpec as P

MESH = pl.DeviceIdType.MESH
BF16 = jnp.bfloat16
F32 = jnp.float32

PLACE = {0: 0, 1: 1, 7: 2, 2: 3, 6: 4, 3: 5, 5: 6, 4: 7}
STEP_PLACES = ((0, 3), (3, 2), (5, 2), (7, 1))

ORDER = (
    ("A",), ("J",), ("Z", 1, 0, "R"), ("Z", 1, 0, "L"), ("C", 0), ("Z", 1, 1, "R"), ("Z", 1, 1, "L"), ("S", 1, 0),
    ("Z", 2, 0, "R"), ("Z", 2, 0, "L"), ("Z", 1, 2, "R"), ("Z", 1, 2, "L"), ("S", 1, 1), ("Z", 3, 0, "R"),
    ("Z", 3, 0, "L"), ("D", 0), ("Z", 2, 1, "R"), ("Z", 2, 1, "L"), ("S", 2, 0), ("Z", 1, 3, "R"),
    ("Z", 1, 3, "L"), ("S", 1, 2), ("Z", 3, 1, "R"), ("Z", 3, 1, "L"), ("S", 3, 0), ("Z", 2, 2, "R"), ("S", 2, 1),
    ("Z", 2, 2, "L"), ("S", 1, 3), ("E", 0), ("Z", 3, 2, "R"), ("C", 1), ("Z", 3, 2, "L"), ("S", 3, 1),
    ("Z", 2, 3, "R"), ("S", 2, 2), ("Z", 2, 3, "L"), ("Z", 3, 3, "R"), ("S", 3, 2), ("Z", 3, 3, "L"), ("S", 2, 3),
    ("F", 0), ("S", 3, 3), ("C", 2), ("R", 0, 0, "R"), ("R", 0, 0, "L"), ("D", 1), ("C", 3), ("R", 0, 1, "R"),
    ("R", 0, 1, "L"), ("D", 2), ("R", 0, 2, "R"), ("R", 0, 2, "L"), ("E", 1), ("R", 0, 3, "R"), ("R", 0, 3, "L"),
    ("D", 3), ("H", 0), ("E", 2), ("F", 1), ("E", 3), ("R", 1, 0, "R"), ("R", 1, 0, "L"), ("F", 2),
    ("R", 1, 1, "R"), ("R", 1, 1, "L"), ("R", 2, 0, "R"), ("R", 2, 0, "L"), ("F", 3), ("R", 2, 1, "R"),
    ("R", 2, 1, "L"), ("W", 0), ("W", 1), ("R", 3, 0, "R"), ("R", 3, 0, "L"), ("W", 2), ("R", 2, 2, "R"),
    ("R", 2, 2, "L"), ("W", 3), ("R", 3, 1, "R"), ("R", 3, 1, "L"), ("W", 4), ("R", 1, 2, "R"), ("R", 1, 2, "L"),
    ("R", 2, 3, "R"), ("R", 2, 3, "L"), ("R", 3, 2, "R"), ("R", 3, 2, "L"), ("R", 1, 3, "R"), ("R", 1, 3, "L"),
    ("H", 2), ("R", 3, 3, "R"), ("R", 3, 3, "L"), ("H", 1), ("H", 3), ("FIN",),
)


def gelu_both(pre_value, grad_value):
    square = pre_value * pre_value
    tanh_part = jnp.tanh(0.7978845608 * (pre_value + 0.044715 * square * pre_value))
    inner_slope = 0.7978845608 * (1.0 + 0.134145 * square)
    value = 0.5 * pre_value * (1.0 + tanh_part)
    slope = 0.5 * (1.0 + tanh_part) + 0.5 * pre_value * (1.0 - tanh_part * tanh_part) * inner_slope
    return value, grad_value * slope


def rows_of(place, count=1):
    return pl.ds(place * 16, count * 16)


def times(left, right):
    return jnp.dot(left, right, preferred_element_type=F32)


def times_transposed(left, right):
    return lax.dot_general(left, right, (((1,), (1,)), ((), ())), preferred_element_type=F32)


def kernel(
    tokens, weight_in, weight_out, grad_out,
    layer_out, grad_tokens, grad_weight_in, grad_weight_out,
    TK, X, WI, WO, PS, PR, YS, YR, HC, HT, GT, SS, SR, OP, ZS, ZR, FS, FR, FO, OB, GI, GO, XA, XB, YT,
    local_sem, a_send, a_recv, j_send, j_recv, c_send, c_recv, z_send, z_recv,
    p_send, p_recv, y_send, y_recv, h_send, h_recv, s_send, s_recv, r_send, r_recv, f_send, f_recv,
):
    dp = lax.axis_index("dp")
    row = lax.axis_index("row")
    z = lax.axis_index("col")
    y, core = dp // 2, dp % 2
    half, x = row // 4, row % 4

    def device(y=y, core=core, half=half, x=x, z=z):
        return {"dp": y * 2 + core, "row": half * 4 + x, "col": z}

    sibling = device(core=1 - core)
    ring = {"R": device(z=(z + 1) % 8), "L": device(z=(z + 7) % 8)}
    across = device(half=1 - half)
    y_peer = {1: device(y=y + 1 - 2 * (y % 2)), 2: device(y=(y + 2) % 4), 3: device(y=3 - y)}
    x_at = {m: (x + m) % 4 for m in (1, 2, 3)}
    x_peer = {m: device(x=x_at[m]) for m in (1, 2, 3)}

    def along_y(step):
        place = (half * 4 + y + step) % 8
        return device(y=place % 4, half=place // 4)

    pending = []
    waited = set()

    def send(src, dst, sems, index, to):
        copy = pltpu.make_async_remote_copy(
            src_ref=src, dst_ref=dst, send_sem=sems[0].at[index], recv_sem=sems[1].at[index],
            device_id=to, device_id_type=MESH,
        )
        copy.start()
        pending.append(copy)

    def arrived(dst, sems, index):
        if (id(sems), index) in waited:
            return
        waited.add((id(sems), index))
        pltpu.make_async_remote_copy(
            src_ref=dst, dst_ref=dst, send_sem=sems[0].at[index], recv_sem=sems[1].at[index],
            device_id=sibling, device_id_type=MESH,
        ).wait_recv()

    a_sem, j_sem, c_sem, z_sem = (a_send, a_recv), (j_send, j_recv), (c_send, c_recv), (z_send, z_recv)
    p_sem, y_sem, h_sem, s_sem = (p_send, p_recv), (y_send, y_recv), (h_send, h_recv), (s_send, s_recv)
    r_sem, f_sem = (r_send, r_recv), (f_send, f_recv)

    fetch = [
        pltpu.make_async_copy(tokens, TK.at[0], local_sem.at[0]),
        pltpu.make_async_copy(grad_out, TK.at[1], local_sem.at[1]),
        pltpu.make_async_copy(weight_in, WI, local_sem.at[2]),
        pltpu.make_async_copy(weight_out, WO, local_sem.at[3]),
    ]
    for copy in fetch:
        copy.start()

    barrier = pltpu.get_barrier_semaphore()
    peers = [sibling, *ring.values(), *y_peer.values(), *x_peer.values()]
    peers += [across]
    for peer in peers:
        pl.semaphore_signal(barrier, inc=1, device_id=peer, device_id_type=MESH)
    pl.semaphore_wait(barrier, len(peers))
    fetch[0].wait()
    fetch[1].wait()

    def do_a():
        for j in (1, 2, 3):
            send(TK.at[:, z], X.at[j, :, rows_of(0)], a_sem, j - 1, y_peer[j])

    def do_j():
        for r in range(8):
            for a in range(2):
                X[0, a, rows_of(PLACE[r])] = TK[a, (z + r) % 8]
        send(X.at[0, :, 0:128], X.at[0, :, 128:256], j_sem, 0, sibling)

    def z_index(j, s, d, a):
        return (((j - 1) * 4 + s) * 2 + "RL".index(d)) * 2 + a

    def z_arrays(s, d):
        return (0, 1) if s < 3 else (("RL".index(d)),)

    def z_arrived(j, s, d):
        place = PLACE[7 - s if d == "R" else s + 1]
        for a in z_arrays(s, d):
            arrived(X.at[j, a, rows_of(place)], z_sem, z_index(j, s, d, a))

    def do_z(j, s, d):
        if s == 0:
            arrived(X.at[j, :, rows_of(0)], a_sem, j - 1)
        place = PLACE[(8 - s) % 8 if d == "R" else s]
        to = PLACE[7 - s if d == "R" else s + 1]
        arrays = z_arrays(s, d)
        if s == 0:
            arrays = (0, 1) if d == "R" else (1, 0)
        for a in z_arrays(s - 1, d) if s else ():
            arrived(X.at[j, a, rows_of(PLACE[8 - s if d == "R" else s])], z_sem, z_index(j, s - 1, d, a))
            if a in arrays:
                send(X.at[j, a, rows_of(place)], X.at[j, a, rows_of(to)], z_sem, z_index(j, s, d, a), ring[d])
        if s == 0:
            for a in arrays:
                send(X.at[j, a, rows_of(place)], X.at[j, a, rows_of(to)], z_sem, z_index(j, s, d, a), ring[d])

    def do_s(j, s):
        z_arrived(j, s, "R")
        z_arrived(j, s, "L")
        q, n = STEP_PLACES[s]
        send(X.at[j, :, rows_of(q, n)], X.at[j, :, rows_of(8 + q, n)], c_sem, (j - 1) * 4 + s, sibling)

    def do_c(j):
        if j == 0:
            arrived(X.at[0, :, 128:256], j_sem, 0)
        else:
            for s in range(4):
                q, n = STEP_PLACES[s]
                arrived(X.at[j, :, rows_of(8 + q, n)], c_sem, (j - 1) * 4 + s)
        PS[:, j, 0] = times(X[j, 0], WI[...]).astype(BF16).reshape(4, 64, 384)
        for m in (2, 1, 3):
            send(PS.at[x_at[m], j, 0], PR.at[m - 1, j, 0], p_sem, j * 6 + m - 1, x_peer[m])
        PS[:, j, 1] = times_transposed(X[j, 1], WO[...]).astype(BF16).reshape(4, 64, 384)
        for m in (2, 1, 3):
            send(PS.at[x_at[m], j, 1], PR.at[m - 1, j, 1], p_sem, j * 6 + m + 2, x_peer[m])

    def do_d(j):
        for a in (0, 1):
            parts = (0, 1, 2)
            for m in (1, 2, 3):
                arrived(PR.at[m - 1, j, a], p_sem, j * 6 + a * 3 + m - 1)
            total = PS[x, j, a].astype(F32)
            for part in parts:
                total = total + PR[part, j, a].astype(F32)
            YS[j, a] = total.astype(BF16)
            send(YS.at[j, a], YR.at[j, a], y_sem, j * 4 + a, across)

    def h_index(j, d, second):
        return (j * 2 + "RL".index(d)) * 2 + second

    def do_e(j):
        for a in (0, 1):
            arrived(YR.at[j, a], y_sem, j * 4 + a)
        pre, grad = (YS[j, a].astype(F32) + YR[j, a].astype(F32) for a in (0, 1))
        value, slope = gelu_both(pre, grad)
        HC[j, 0, x] = value.astype(BF16)
        HC[j, 1, x] = slope.astype(BF16)
        for m in (2, 1, 3):
            send(HC.at[j, :, x], HC.at[j, :, x], h_sem, j * 4 + m, x_peer[m])

    def do_f(j):
        for m in (1, 2, 3):
            arrived(HC.at[j, :, x_at[4 - m]], h_sem, j * 4 + m)
        for a in (0, 1):
            lhs = HC[j, a].reshape(256, 384)
            val = times(lhs, WO[...]) if a == 0 else times_transposed(lhs, WI[...])
            OP[j, a] = val[0:128]
            SS[j, a] = val[128:256].astype(BF16)
        for part, (q, n) in enumerate(((5, 3), (0, 5))):
            send(SS.at[j, :, rows_of(q, n)], SR.at[j, :, rows_of(q, n)], s_sem, j * 2 + part, sibling)
        HT[:, j * 256:(j + 1) * 256] = HC[j, 0].reshape(256, 384).T
        GT[:, j * 256:(j + 1) * 256] = HC[j, 1].reshape(256, 384).T

    def r_index(j, i, d):
        return (j * 4 + i) * 2 + "RL".index(d)

    def r_ref(buffer, j, i, d):
        direction = "RL".index(d)
        if i == 0:
            return buffer.at[j, i, direction, direction]
        return buffer.at[j, i, direction]

    def both_cores(j, r, a):
        rows = rows_of(PLACE[r])
        return OP[j, a, rows] + SR[j, a, rows].astype(F32)

    def received(j, i, d, a):
        return ZR[j, i, "RL".index(d), a].astype(F32)

    def do_r(j, i, d):
        direction = "RL".index(d)
        q, n = ((5, 3), (0, 5))[i // 2]
        arrived(SR.at[j, :, rows_of(q, n)], s_sem, j * 2 + i // 2)
        r = 4 - i if d == "R" else 4 + i
        if i:
            arrived(r_ref(ZR, j, i - 1, d), r_sem, r_index(j, i - 1, d))
        for a in (0, 1) if i else (direction,):
            total = both_cores(j, r, a)
            if i > 1 or (i == 1 and a == direction):
                total = total + received(j, i - 1, d, a)
            ZS[j, i, direction, a] = total.astype(BF16)
        send(r_ref(ZS, j, i, d), r_ref(ZR, j, i, d), r_sem, r_index(j, i, d), ring[d])

    def do_h(j):
        arrived(SR.at[j, :, rows_of(0, 5)], s_sem, j * 2 + 1)
        for d in "RL":
            arrived(r_ref(ZR, j, 3, d), r_sem, r_index(j, 3, d))
        for a in (0, 1):
            total = both_cores(j, 0, a) + received(j, 3, "R", a) + received(j, 3, "L", a)
            if j == 0:
                FO[a] = total
            else:
                FS[j - 1, a] = total.astype(BF16)
        if j:
            send(FS.at[j - 1], FR.at[j - 1], f_sem, j - 1, y_peer[j])

    def do_w(k):
        cols = pl.ds(k * 256, min(256, 1152 - k * 256))
        GI[cols, :] = times(GT[...], X[:, 0, :, cols].reshape(1024, cols.size)).T.astype(BF16)
        GO[:, cols] = times(HT[...], X[:, 1, :, cols].reshape(1024, cols.size)).astype(BF16)

    def do_fin():
        stores = [
            pltpu.make_async_copy(GI, grad_weight_in, local_sem.at[4]),
            pltpu.make_async_copy(GO, grad_weight_out, local_sem.at[5]),
        ]
        for copy in stores:
            copy.start()
        total = FO[...]
        for j in (1, 2, 3):
            arrived(FR.at[j - 1], f_sem, j - 1)
            total = total + FR[j - 1].astype(F32)
        OB[...] = total.astype(BF16)
        stores.append(pltpu.make_async_copy(OB.at[0], layer_out, local_sem.at[6]))
        stores.append(pltpu.make_async_copy(OB.at[1], grad_tokens, local_sem.at[7]))
        stores[2].start()
        stores[3].start()
        for copy in pending:
            copy.wait_send()
        for copy in stores:
            copy.wait()

    steps = {
        "A": do_a, "J": do_j, "Z": do_z, "S": do_s, "C": do_c, "D": do_d, "E": do_e, "F": do_f,
        "R": do_r, "H": do_h, "W": do_w, "FIN": do_fin,
    }
    weights_here = False
    for step in ORDER:
        if step[0] == "C" and not weights_here:
            fetch[2].wait()
            fetch[3].wait()
            weights_here = True
        steps[step[0]](*step[1:])


def hand_out(*refs):
    copies = [
        pltpu.make_async_copy(refs[i], refs[4 + i], refs[8].at[i]) for i in (2, 3, 0, 1)
    ]
    for copy in copies:
        copy.start()
    for copy in copies:
        copy.wait()


def shards(tokens, weight_in, weight_out, grad_out):
    any_space = pl.BlockSpec(memory_space=pl.ANY)
    dma = pltpu.SemaphoreType.DMA
    shapes = (
        jax.ShapeDtypeStruct((16, 1152), BF16),
        jax.ShapeDtypeStruct((16, 1152), BF16),
        jax.ShapeDtypeStruct((1152, 384), BF16),
        jax.ShapeDtypeStruct((384, 1152), BF16),
    )
    results = pl.pallas_call(
        kernel,
        out_shape=shapes,
        in_specs=[any_space] * 4,
        out_specs=(any_space,) * 4,
        scratch_shapes=[
            pltpu.VMEM((2, 8, 16, 1152), BF16),
            pltpu.VMEM((4, 2, 256, 1152), BF16),
            pltpu.VMEM((1152, 384), BF16),
            pltpu.VMEM((384, 1152), BF16),
            pltpu.VMEM((4, 4, 2, 64, 384), BF16),
            pltpu.VMEM((3, 4, 2, 64, 384), BF16),
            pltpu.VMEM((4, 2, 64, 384), BF16),
            pltpu.VMEM((4, 2, 64, 384), BF16),
            pltpu.VMEM((4, 2, 4, 64, 384), BF16),
            pltpu.VMEM((384, 1024), BF16),
            pltpu.VMEM((384, 1024), BF16),
            pltpu.VMEM((4, 2, 128, 1152), BF16),
            pltpu.VMEM((4, 2, 128, 1152), BF16),
            pltpu.VMEM((4, 2, 128, 1152), F32),
            pltpu.VMEM((4, 4, 2, 2, 16, 1152), BF16),
            pltpu.VMEM((4, 4, 2, 2, 16, 1152), BF16),
            pltpu.VMEM((3, 2, 16, 1152), BF16),
            pltpu.VMEM((3, 2, 16, 1152), BF16),
            pltpu.VMEM((2, 16, 1152), F32),
            pltpu.VMEM((2, 16, 1152), BF16),
            pltpu.VMEM((1152, 384), BF16),
            pltpu.VMEM((384, 1152), BF16),
            pltpu.VMEM((4, 2, 64, 384), BF16),
            pltpu.VMEM((4, 2, 64, 384), BF16),
            pltpu.VMEM((4, 2, 64, 384), BF16),
            dma((8,)),
            dma((3,)), dma((3,)),
            dma((1,)), dma((1,)),
            dma((12,)), dma((12,)),
            dma((48,)), dma((48,)),
            dma((24,)), dma((24,)),
            dma((16,)), dma((16,)),
            dma((16,)), dma((16,)),
            dma((8,)), dma((8,)),
            dma((32,)), dma((32,)),
            dma((3,)), dma((3,)),
        ],
        compiler_params=pltpu.CompilerParams(
            collective_id=0, has_side_effects=True, vmem_limit_bytes=56 * 1024 * 1024
        ),
        cost_estimate=pl.CostEstimate(flops=5436000000, bytes_accessed=8000000, transcendentals=1000000),
    )(tokens.reshape(8, 16, 1152), weight_in, weight_out, grad_out.reshape(8, 16, 1152))
    return pl.pallas_call(
        hand_out,
        out_shape=shapes,
        in_specs=[any_space] * 4,
        out_specs=(any_space,) * 4,
        scratch_shapes=[dma((4,))],
    )(*results)


def solution(mesh):
    placed = (P("dp", "row"), P("row", ("dp", "col")), P(("dp", "col"), "row"), P("dp", "row"))
    return jax.shard_map(
        shards,
        mesh=mesh,
        in_specs=placed,
        out_specs=(
            P(("dp", "col"), "row"),
            P(("dp", "col"), "row"),
            P("row", ("dp", "col")),
            P(("dp", "col"), "row"),
        ),
        check_vma=False,
    )
```

```python
import jax
import jax.numpy as jnp
from jax import lax
from jax.experimental import pallas as pl
from jax.experimental.pallas import tpu as pltpu
from jax.sharding import PartitionSpec as P

MESH = pl.DeviceIdType.MESH
BF16 = jnp.bfloat16
F32 = jnp.float32

PLACE = {0: 0, 1: 1, 7: 2, 2: 3, 6: 4, 3: 5, 5: 6, 4: 7}
STEP_PLACES = ((0, 3), (3, 2), (5, 2), (7, 1))

ORDER = (
    ("A",), ("J",), ("Z", 1, 0, "R"), ("Z", 1, 0, "L"), ("C", 0), ("Z", 1, 1, "R"), ("Z", 1, 1, "L"), ("S", 1, 0),
    ("Z", 2, 0, "R"), ("Z", 2, 0, "L"), ("X2", 0, "R"), ("X2", 0, "L"), ("Z", 1, 2, "R"), ("Z", 1, 2, "L"),
    ("S", 1, 1), ("D", 0), ("Z", 3, 0, "R"), ("Z", 3, 0, "L"), ("Z", 2, 1, "R"), ("Z", 2, 1, "L"), ("S", 2, 0),
    ("Y2", 0, "p"), ("Z", 1, 3, "R"), ("Z", 1, 3, "L"), ("Y2", 0, "m"), ("S", 1, 2), ("Z", 3, 1, "R"),
    ("Z", 3, 1, "L"), ("S", 3, 0), ("Z", 2, 2, "R"), ("S", 2, 1), ("Z", 2, 2, "L"), ("S", 1, 3), ("E", 0),
    ("Z", 3, 2, "R"), ("Z", 3, 2, "L"), ("S", 3, 1), ("C", 1), ("Z", 2, 3, "R"), ("S", 2, 2), ("Z", 2, 3, "L"),
    ("Z", 3, 3, "R"), ("S", 3, 2), ("Z", 3, 3, "L"), ("G2", 0, "R"), ("G2", 0, "L"), ("S", 2, 3), ("X2", 1, "R"),
    ("X2", 1, "L"), ("S", 3, 3), ("C", 2), ("F", 0), ("D", 1), ("C", 3), ("X2", 2, "R"), ("X2", 2, "L"),
    ("R", 0, 0, "R"), ("R", 0, 0, "L"), ("Y2", 1, "p"), ("Y2", 1, "m"), ("X2", 3, "R"), ("X2", 3, "L"),
    ("R", 0, 1, "R"), ("R", 0, 1, "L"), ("D", 2), ("D", 3), ("R", 0, 2, "R"), ("R", 0, 2, "L"), ("E", 1),
    ("Y2", 2, "p"), ("Y2", 2, "m"), ("Y2", 3, "p"), ("Y2", 3, "m"), ("R", 0, 3, "R"), ("R", 0, 3, "L"),
    ("G2", 1, "R"), ("G2", 1, "L"), ("H", 0), ("E", 2), ("F", 1), ("E", 3), ("G2", 2, "R"), ("G2", 2, "L"),
    ("R", 1, 0, "R"), ("R", 1, 0, "L"), ("R", 1, 1, "R"), ("R", 1, 1, "L"), ("G2", 3, "R"), ("G2", 3, "L"),
    ("F", 2), ("R", 1, 2, "R"), ("R", 1, 2, "L"), ("F", 3), ("W", 0), ("R", 2, 0, "R"), ("R", 2, 0, "L"), ("W", 1),
    ("R", 3, 0, "R"), ("R", 3, 0, "L"), ("R", 1, 3, "R"), ("R", 1, 3, "L"), ("W", 2), ("R", 2, 1, "R"),
    ("R", 2, 1, "L"), ("W", 3), ("R", 3, 1, "R"), ("R", 3, 1, "L"), ("W", 4), ("H", 1), ("R", 2, 2, "R"),
    ("R", 2, 2, "L"), ("R", 3, 2, "R"), ("R", 3, 2, "L"), ("R", 2, 3, "R"), ("R", 2, 3, "L"), ("R", 3, 3, "R"),
    ("R", 3, 3, "L"), ("H", 2), ("H", 3), ("FIN",),
)


def gelu_both(pre_value, grad_value):
    square = pre_value * pre_value
    tanh_part = jnp.tanh(0.7978845608 * (pre_value + 0.044715 * square * pre_value))
    inner_slope = 0.7978845608 * (1.0 + 0.134145 * square)
    value = 0.5 * pre_value * (1.0 + tanh_part)
    slope = 0.5 * (1.0 + tanh_part) + 0.5 * pre_value * (1.0 - tanh_part * tanh_part) * inner_slope
    return value, grad_value * slope


def rows_of(place, count=1):
    return pl.ds(place * 16, count * 16)


def times(left, right):
    return jnp.dot(left, right, preferred_element_type=F32)


def times_transposed(left, right):
    return lax.dot_general(left, right, (((1,), (1,)), ((), ())), preferred_element_type=F32)


def kernel(
    tokens, weight_in, weight_out, grad_out,
    layer_out, grad_tokens, grad_weight_in, grad_weight_out,
    TK, X, WI, WO, PS, PR, YS, YR, HC, HT, GT, SS, SR, OP, ZS, ZR, FS, FR, FO, OB, GI, GO, XA, XB, YT,
    local_sem, a_send, a_recv, j_send, j_recv, c_send, c_recv, z_send, z_recv,
    p_send, p_recv, y_send, y_recv, h_send, h_recv, s_send, s_recv, r_send, r_recv, f_send, f_recv,
):
    dp = lax.axis_index("dp")
    row = lax.axis_index("row")
    z = lax.axis_index("col")
    y, core = dp // 2, dp % 2
    half, x = row // 4, row % 4

    def device(y=y, core=core, half=half, x=x, z=z):
        return {"dp": y * 2 + core, "row": half * 4 + x, "col": z}

    sibling = device(core=1 - core)
    ring = {"R": device(z=(z + 1) % 8), "L": device(z=(z + 7) % 8)}
    across = device(half=1 - half)
    y_peer = {1: device(y=y + 1 - 2 * (y % 2)), 2: device(y=(y + 2) % 4), 3: device(y=3 - y)}
    x_at = {m: (x + m) % 4 for m in (1, 2, 3)}
    x_peer = {m: device(x=x_at[m]) for m in (1, 2, 3)}

    def along_y(step):
        place = (half * 4 + y + step) % 8
        return device(y=place % 4, half=place // 4)

    pending = []
    waited = set()

    def send(src, dst, sems, index, to):
        copy = pltpu.make_async_remote_copy(
            src_ref=src, dst_ref=dst, send_sem=sems[0].at[index], recv_sem=sems[1].at[index],
            device_id=to, device_id_type=MESH,
        )
        copy.start()
        pending.append(copy)

    def arrived(dst, sems, index):
        if (id(sems), index) in waited:
            return
        waited.add((id(sems), index))
        pltpu.make_async_remote_copy(
            src_ref=dst, dst_ref=dst, send_sem=sems[0].at[index], recv_sem=sems[1].at[index],
            device_id=sibling, device_id_type=MESH,
        ).wait_recv()

    a_sem, j_sem, c_sem, z_sem = (a_send, a_recv), (j_send, j_recv), (c_send, c_recv), (z_send, z_recv)
    p_sem, y_sem, h_sem, s_sem = (p_send, p_recv), (y_send, y_recv), (h_send, h_recv), (s_send, s_recv)
    r_sem, f_sem = (r_send, r_recv), (f_send, f_recv)

    fetch = [
        pltpu.make_async_copy(tokens, TK.at[0], local_sem.at[0]),
        pltpu.make_async_copy(grad_out, TK.at[1], local_sem.at[1]),
        pltpu.make_async_copy(weight_in, WI, local_sem.at[2]),
        pltpu.make_async_copy(weight_out, WO, local_sem.at[3]),
    ]
    for copy in fetch:
        copy.start()

    barrier = pltpu.get_barrier_semaphore()
    peers = [sibling, *ring.values(), *y_peer.values(), *x_peer.values()]
    peers += [along_y(step) for step in (1, 3, 5, 7)]
    for peer in peers:
        pl.semaphore_signal(barrier, inc=1, device_id=peer, device_id_type=MESH)
    pl.semaphore_wait(barrier, len(peers))
    fetch[0].wait()
    fetch[1].wait()

    def do_a():
        for j in (1, 2, 3):
            send(TK.at[:, z], X.at[j, :, rows_of(0)], a_sem, j - 1, y_peer[j])

    def do_j():
        for r in range(8):
            for a in range(2):
                X[0, a, rows_of(PLACE[r])] = TK[a, (z + r) % 8]
        send(X.at[0, :, 0:128], X.at[0, :, 128:256], j_sem, 0, sibling)

    def z_index(j, s, d, a):
        return (((j - 1) * 4 + s) * 2 + "RL".index(d)) * 2 + a

    def z_arrays(s, d):
        return (0, 1) if s < 3 else (("RL".index(d)),)

    def z_arrived(j, s, d):
        place = PLACE[7 - s if d == "R" else s + 1]
        for a in z_arrays(s, d):
            arrived(X.at[j, a, rows_of(place)], z_sem, z_index(j, s, d, a))

    def do_z(j, s, d):
        if s == 0:
            arrived(X.at[j, :, rows_of(0)], a_sem, j - 1)
        place = PLACE[(8 - s) % 8 if d == "R" else s]
        to = PLACE[7 - s if d == "R" else s + 1]
        arrays = z_arrays(s, d)
        if s == 0:
            arrays = (0, 1) if d == "R" else (1, 0)
        for a in z_arrays(s - 1, d) if s else ():
            arrived(X.at[j, a, rows_of(PLACE[8 - s if d == "R" else s])], z_sem, z_index(j, s - 1, d, a))
            if a in arrays:
                send(X.at[j, a, rows_of(place)], X.at[j, a, rows_of(to)], z_sem, z_index(j, s, d, a), ring[d])
        if s == 0:
            for a in arrays:
                send(X.at[j, a, rows_of(place)], X.at[j, a, rows_of(to)], z_sem, z_index(j, s, d, a), ring[d])

    def do_s(j, s):
        z_arrived(j, s, "R")
        z_arrived(j, s, "L")
        q, n = STEP_PLACES[s]
        send(X.at[j, :, rows_of(q, n)], X.at[j, :, rows_of(8 + q, n)], c_sem, (j - 1) * 4 + s, sibling)

    def do_c(j):
        if j == 0:
            arrived(X.at[0, :, 128:256], j_sem, 0)
        else:
            for s in range(4):
                q, n = STEP_PLACES[s]
                arrived(X.at[j, :, rows_of(8 + q, n)], c_sem, (j - 1) * 4 + s)
        PS[:, j, 0] = times(X[j, 0], WI[...]).astype(BF16).reshape(4, 64, 384)
        send(PS.at[x_at[2], j, 0], XA.at[j, 0], p_sem, j * 6, x_peer[1])
        send(PS.at[x_at[3], j, 0], PR.at[0, j, 0], p_sem, j * 6 + 1, x_peer[3])
        PS[:, j, 1] = times_transposed(X[j, 1], WO[...]).astype(BF16).reshape(4, 64, 384)
        send(PS.at[x_at[2], j, 1], XA.at[j, 1], p_sem, j * 6 + 2, x_peer[3])
        send(PS.at[x_at[1], j, 1], PR.at[0, j, 1], p_sem, j * 6 + 3, x_peer[1])

    def do_x2(j, d):
        a, m = (0, 1) if d == "R" else (1, 3)
        arrived(XA.at[j, a], p_sem, j * 6 + a * 2)
        XB[j, a] = (PS[x_at[m], j, a].astype(F32) + XA[j, a].astype(F32)).astype(BF16)
        send(XB.at[j, a], PR.at[1, j, a], p_sem, j * 6 + 4 + a, x_peer[m])

    def do_d(j):
        for a in (0, 1):
            arrived(PR.at[0, j, a], p_sem, j * 6 + a * 2 + 1)
            arrived(PR.at[1, j, a], p_sem, j * 6 + 4 + a)
            parts = (0, 1)
            total = PS[x, j, a].astype(F32)
            for part in parts:
                total = total + PR[part, j, a].astype(F32)
            YS[j, a] = total.astype(BF16)
            send(YS.at[j, a], YT.at[j, a], y_sem, j * 4 + a, along_y((1, 7)[a]))

    def do_y2(j, d):
        a = "pm".index(d)
        arrived(YT.at[j, a], y_sem, j * 4 + a)
        send(YT.at[j, a], YR.at[j, a], y_sem, j * 4 + 2 + a, along_y((3, 5)[a]))

    def h_index(j, d, second):
        return (j * 2 + "RL".index(d)) * 2 + second

    def do_e(j):
        for a in (0, 1):
            arrived(YR.at[j, a], y_sem, j * 4 + 2 + a)
        pre, grad = (YS[j, a].astype(F32) + YR[j, a].astype(F32) for a in (0, 1))
        value, slope = gelu_both(pre, grad)
        HC[j, 0, x] = value.astype(BF16)
        HC[j, 1, x] = slope.astype(BF16)
        for d, m in (("R", 1), ("L", 3)):
            send(HC.at[j, :, x], HC.at[j, :, x], h_sem, h_index(j, d, 0), x_peer[m])

    def do_g2(j, d):
        m, a = (3, 0) if d == "R" else (1, 1)
        arrived(HC.at[j, :, x_at[m]], h_sem, h_index(j, d, 0))
        send(HC.at[j, a, x_at[m]], HC.at[j, a, x_at[m]], h_sem, h_index(j, d, 1), x_peer[4 - m])

    def do_f(j):
        for a, d in ((0, "R"), (1, "L")):
            arrived(HC.at[j, a, x_at[2]], h_sem, h_index(j, d, 1))
        for a in (0, 1):
            lhs = HC[j, a].reshape(256, 384)
            val = times(lhs, WO[...]) if a == 0 else times_transposed(lhs, WI[...])
            OP[j, a] = val[0:128]
            SS[j, a] = val[128:256].astype(BF16)
        for part, (q, n) in enumerate(((5, 3), (0, 5))):
            send(SS.at[j, :, rows_of(q, n)], SR.at[j, :, rows_of(q, n)], s_sem, j * 2 + part, sibling)
        HT[:, j * 256:(j + 1) * 256] = HC[j, 0].reshape(256, 384).T
        GT[:, j * 256:(j + 1) * 256] = HC[j, 1].reshape(256, 384).T

    def r_index(j, i, d):
        return (j * 4 + i) * 2 + "RL".index(d)

    def r_ref(buffer, j, i, d):
        direction = "RL".index(d)
        if i == 0:
            return buffer.at[j, i, direction, direction]
        return buffer.at[j, i, direction]

    def both_cores(j, r, a):
        rows = rows_of(PLACE[r])
        return OP[j, a, rows] + SR[j, a, rows].astype(F32)

    def received(j, i, d, a):
        return ZR[j, i, "RL".index(d), a].astype(F32)

    def do_r(j, i, d):
        direction = "RL".index(d)
        q, n = ((5, 3), (0, 5))[i // 2]
        arrived(SR.at[j, :, rows_of(q, n)], s_sem, j * 2 + i // 2)
        r = 4 - i if d == "R" else 4 + i
        if i:
            arrived(r_ref(ZR, j, i - 1, d), r_sem, r_index(j, i - 1, d))
        for a in (0, 1) if i else (direction,):
            total = both_cores(j, r, a)
            if i > 1 or (i == 1 and a == direction):
                total = total + received(j, i - 1, d, a)
            ZS[j, i, direction, a] = total.astype(BF16)
        send(r_ref(ZS, j, i, d), r_ref(ZR, j, i, d), r_sem, r_index(j, i, d), ring[d])

    def do_h(j):
        arrived(SR.at[j, :, rows_of(0, 5)], s_sem, j * 2 + 1)
        for d in "RL":
            arrived(r_ref(ZR, j, 3, d), r_sem, r_index(j, 3, d))
        for a in (0, 1):
            total = both_cores(j, 0, a) + received(j, 3, "R", a) + received(j, 3, "L", a)
            if j == 0:
                FO[a] = total
            else:
                FS[j - 1, a] = total.astype(BF16)
        if j:
            send(FS.at[j - 1], FR.at[j - 1], f_sem, j - 1, y_peer[j])

    def do_w(k):
        cols = pl.ds(k * 256, min(256, 1152 - k * 256))
        GI[cols, :] = times(GT[...], X[:, 0, :, cols].reshape(1024, cols.size)).T.astype(BF16)
        GO[:, cols] = times(HT[...], X[:, 1, :, cols].reshape(1024, cols.size)).astype(BF16)

    def do_fin():
        stores = [
            pltpu.make_async_copy(GI, grad_weight_in, local_sem.at[4]),
            pltpu.make_async_copy(GO, grad_weight_out, local_sem.at[5]),
        ]
        for copy in stores:
            copy.start()
        total = FO[...]
        for j in (1, 2, 3):
            arrived(FR.at[j - 1], f_sem, j - 1)
            total = total + FR[j - 1].astype(F32)
        OB[...] = total.astype(BF16)
        stores.append(pltpu.make_async_copy(OB.at[0], layer_out, local_sem.at[6]))
        stores.append(pltpu.make_async_copy(OB.at[1], grad_tokens, local_sem.at[7]))
        stores[2].start()
        stores[3].start()
        for copy in pending:
            copy.wait_send()
        for copy in stores:
            copy.wait()

    steps = {
        "A": do_a, "J": do_j, "Z": do_z, "S": do_s, "C": do_c, "D": do_d, "E": do_e, "F": do_f,
        "R": do_r, "H": do_h, "W": do_w, "FIN": do_fin,
    }
    steps.update({"X2": do_x2, "G2": do_g2})
    steps["Y2"] = do_y2
    weights_here = False
    for step in ORDER:
        if step[0] == "C" and not weights_here:
            fetch[2].wait()
            fetch[3].wait()
            weights_here = True
        steps[step[0]](*step[1:])


def hand_out(*refs):
    results, outputs, held, arrive, leave = refs[0:4], refs[4:8], refs[8:12], refs[12], refs[13]
    order = (2, 3, 0, 1)
    fetches = {i: pltpu.make_async_copy(results[i], held[i], arrive.at[i]) for i in order}
    stores = {i: pltpu.make_async_copy(held[i], outputs[i], leave.at[i]) for i in order}
    for i in order:
        fetches[i].start()
    for i in order:
        fetches[i].wait()
        stores[i].start()
    for i in order:
        stores[i].wait()


def shards(tokens, weight_in, weight_out, grad_out):
    any_space = pl.BlockSpec(memory_space=pl.ANY)
    dma = pltpu.SemaphoreType.DMA
    shapes = (
        jax.ShapeDtypeStruct((16, 1152), BF16),
        jax.ShapeDtypeStruct((16, 1152), BF16),
        jax.ShapeDtypeStruct((1152, 384), BF16),
        jax.ShapeDtypeStruct((384, 1152), BF16),
    )
    results = pl.pallas_call(
        kernel,
        out_shape=shapes,
        in_specs=[any_space] * 4,
        out_specs=(any_space,) * 4,
        scratch_shapes=[
            pltpu.VMEM((2, 8, 16, 1152), BF16),
            pltpu.VMEM((4, 2, 256, 1152), BF16),
            pltpu.VMEM((1152, 384), BF16),
            pltpu.VMEM((384, 1152), BF16),
            pltpu.VMEM((4, 4, 2, 64, 384), BF16),
            pltpu.VMEM((3, 4, 2, 64, 384), BF16),
            pltpu.VMEM((4, 2, 64, 384), BF16),
            pltpu.VMEM((4, 2, 64, 384), BF16),
            pltpu.VMEM((4, 2, 4, 64, 384), BF16),
            pltpu.VMEM((384, 1024), BF16),
            pltpu.VMEM((384, 1024), BF16),
            pltpu.VMEM((4, 2, 128, 1152), BF16),
            pltpu.VMEM((4, 2, 128, 1152), BF16),
            pltpu.VMEM((4, 2, 128, 1152), F32),
            pltpu.VMEM((4, 4, 2, 2, 16, 1152), BF16),
            pltpu.VMEM((4, 4, 2, 2, 16, 1152), BF16),
            pltpu.VMEM((3, 2, 16, 1152), BF16),
            pltpu.VMEM((3, 2, 16, 1152), BF16),
            pltpu.VMEM((2, 16, 1152), F32),
            pltpu.VMEM((2, 16, 1152), BF16),
            pltpu.VMEM((1152, 384), BF16),
            pltpu.VMEM((384, 1152), BF16),
            pltpu.VMEM((4, 2, 64, 384), BF16),
            pltpu.VMEM((4, 2, 64, 384), BF16),
            pltpu.VMEM((4, 2, 64, 384), BF16),
            dma((8,)),
            dma((3,)), dma((3,)),
            dma((1,)), dma((1,)),
            dma((12,)), dma((12,)),
            dma((48,)), dma((48,)),
            dma((24,)), dma((24,)),
            dma((16,)), dma((16,)),
            dma((16,)), dma((16,)),
            dma((8,)), dma((8,)),
            dma((32,)), dma((32,)),
            dma((3,)), dma((3,)),
        ],
        compiler_params=pltpu.CompilerParams(
            collective_id=0, has_side_effects=True, vmem_limit_bytes=56 * 1024 * 1024
        ),
        cost_estimate=pl.CostEstimate(flops=5436000000, bytes_accessed=8000000, transcendentals=1000000),
    )(tokens.reshape(8, 16, 1152), weight_in, weight_out, grad_out.reshape(8, 16, 1152))
    return pl.pallas_call(
        hand_out,
        out_shape=shapes,
        in_specs=[any_space] * 4,
        out_specs=(any_space,) * 4,
        scratch_shapes=[*(pltpu.VMEM(shape.shape, BF16) for shape in shapes), dma((4,)), dma((4,))],
    )(*results)


def solution(mesh):
    placed = (P("dp", "row"), P("row", ("dp", "col")), P(("dp", "col"), "row"), P("dp", "row"))
    return jax.shard_map(
        shards,
        mesh=mesh,
        in_specs=placed,
        out_specs=(
            P(("dp", "col"), "row"),
            P(("dp", "col"), "row"),
            P("row", ("dp", "col")),
            P(("dp", "col"), "row"),
        ),
        check_vma=False,
    )
```

```python
import jax
import jax.numpy as jnp
from jax import lax
from jax.experimental import pallas as pl
from jax.experimental.pallas import tpu as pltpu
from jax.sharding import PartitionSpec as P

MESH = pl.DeviceIdType.MESH
BF16 = jnp.bfloat16
F32 = jnp.float32

PLACE = {0: 0, 1: 1, 7: 2, 2: 3, 6: 4, 3: 5, 5: 6, 4: 7}
STEPS_OF = ((0, 1), (2, 3))
PLACES_OF = ((0, 5), (5, 3))

ORDER = (
    ("A",), ("J",), ("Z", 1, 0, "R"), ("Z", 1, 0, "L"), ("C", 0), ("Z", 2, 0, "R"), ("Z", 2, 0, "L"),
    ("Z", 1, 1, "R"), ("Z", 1, 1, "L"), ("Z", 3, 0, "R"), ("Z", 3, 0, "L"), ("Z", 2, 1, "R"), ("Z", 2, 1, "L"),
    ("Z", 1, 2, "R"), ("Z", 1, 2, "L"), ("S", 1, 0), ("D", 0), ("Z", 3, 1, "R"), ("Z", 3, 1, "L"),
    ("Z", 2, 2, "R"), ("Z", 2, 2, "L"), ("S", 2, 0), ("Z", 1, 3, "R"), ("Z", 1, 3, "L"), ("Z", 3, 2, "R"),
    ("Z", 3, 2, "L"), ("S", 3, 0), ("Z", 2, 3, "R"), ("Z", 2, 3, "L"), ("S", 1, 1), ("E", 0), ("Z", 3, 3, "R"),
    ("Z", 3, 3, "L"), ("S", 2, 1), ("C", 1), ("S", 3, 1), ("C", 2), ("F", 0), ("C", 3), ("D", 1), ("R", 0, 0, "R"),
    ("R", 0, 0, "L"), ("D", 2), ("R", 0, 1, "R"), ("R", 0, 1, "L"), ("D", 3), ("E", 1), ("R", 0, 2, "R"),
    ("R", 0, 2, "L"), ("E", 2), ("R", 0, 3, "R"), ("R", 0, 3, "L"), ("E", 3), ("F", 1), ("H", 0), ("F", 2),
    ("R", 1, 0, "R"), ("R", 1, 0, "L"), ("F", 3), ("R", 2, 0, "R"), ("R", 2, 0, "L"), ("R", 1, 1, "R"),
    ("R", 1, 1, "L"), ("W", 0), ("R", 3, 0, "R"), ("R", 3, 0, "L"), ("R", 2, 1, "R"), ("R", 2, 1, "L"), ("W", 1),
    ("R", 1, 2, "R"), ("R", 1, 2, "L"), ("R", 3, 1, "R"), ("R", 3, 1, "L"), ("W", 2), ("R", 2, 2, "R"),
    ("R", 2, 2, "L"), ("W", 3), ("R", 1, 3, "R"), ("R", 1, 3, "L"), ("R", 3, 2, "R"), ("R", 3, 2, "L"), ("W", 4),
    ("R", 2, 3, "R"), ("R", 2, 3, "L"), ("H", 1), ("R", 3, 3, "R"), ("R", 3, 3, "L"), ("H", 2), ("H", 3), ("FIN",),
)


def gelu_both(pre_value, grad_value):
    square = pre_value * pre_value
    tanh_part = jnp.tanh(0.7978845608 * (pre_value + 0.044715 * square * pre_value))
    inner_slope = 0.7978845608 * (1.0 + 0.134145 * square)
    value = 0.5 * pre_value * (1.0 + tanh_part)
    slope = 0.5 * (1.0 + tanh_part) + 0.5 * pre_value * (1.0 - tanh_part * tanh_part) * inner_slope
    return value, grad_value * slope


def rows_of(place, count=1):
    return pl.ds(place * 16, count * 16)


def times(left, right):
    return jnp.dot(left, right, preferred_element_type=F32)


def times_transposed(left, right):
    return lax.dot_general(left, right, (((1,), (1,)), ((), ())), preferred_element_type=F32)


def kernel(
    tokens, weight_in, weight_out, grad_out,
    layer_out, grad_tokens, grad_weight_in, grad_weight_out,
    TK, X, WI, WO, PS, PR, YS, YR, HC, HT, GT, SS, SR, OP, ZS, ZR, FS, FR, FO, OB, GI, GO,
    local_sem, a_send, a_recv, j_send, j_recv, c_send, c_recv, z_send, z_recv,
    p_send, p_recv, y_send, y_recv, h_send, h_recv, s_send, s_recv, r_send, r_recv, f_send, f_recv,
):
    dp = lax.axis_index("dp")
    row = lax.axis_index("row")
    z = lax.axis_index("col")
    y, core = dp // 2, dp % 2
    half, x = row // 4, row % 4

    def device(y=y, core=core, half=half, x=x, z=z):
        return {"dp": y * 2 + core, "row": half * 4 + x, "col": z}

    sibling = device(core=1 - core)
    ring = {"R": device(z=(z + 1) % 8), "L": device(z=(z + 7) % 8)}
    across = device(half=1 - half)
    y_peer = {1: device(y=y + 1 - 2 * (y % 2)), 2: device(y=(y + 2) % 4), 3: device(y=3 - y)}
    x_at = {m: (x + m) % 4 for m in (1, 2, 3)}
    x_peer = {m: device(x=x_at[m]) for m in (1, 2, 3)}

    pending = []
    waited = set()

    def send(src, dst, sems, index, to):
        copy = pltpu.make_async_remote_copy(
            src_ref=src, dst_ref=dst, send_sem=sems[0].at[index], recv_sem=sems[1].at[index],
            device_id=to, device_id_type=MESH,
        )
        copy.start()
        pending.append(copy)

    def arrived(dst, sems, index):
        if (id(sems), index) in waited:
            return
        waited.add((id(sems), index))
        pltpu.make_async_remote_copy(
            src_ref=dst, dst_ref=dst, send_sem=sems[0].at[index], recv_sem=sems[1].at[index],
            device_id=sibling, device_id_type=MESH,
        ).wait_recv()

    a_sem, j_sem, c_sem, z_sem = (a_send, a_recv), (j_send, j_recv), (c_send, c_recv), (z_send, z_recv)
    p_sem, y_sem, h_sem, s_sem = (p_send, p_recv), (y_send, y_recv), (h_send, h_recv), (s_send, s_recv)
    r_sem, f_sem = (r_send, r_recv), (f_send, f_recv)

    fetch = [
        pltpu.make_async_copy(tokens, TK.at[0], local_sem.at[0]),
        pltpu.make_async_copy(grad_out, TK.at[1], local_sem.at[1]),
        pltpu.make_async_copy(weight_in, WI, local_sem.at[2]),
        pltpu.make_async_copy(weight_out, WO, local_sem.at[3]),
    ]
    for copy in fetch:
        copy.start()

    barrier = pltpu.get_barrier_semaphore()
    peers = [sibling, *ring.values(), *y_peer.values(), *x_peer.values()]
    peers += [across]
    for peer in peers:
        pl.semaphore_signal(barrier, inc=1, device_id=peer, device_id_type=MESH)
    pl.semaphore_wait(barrier, len(peers))
    fetch[0].wait()
    fetch[1].wait()

    def do_a():
        for j in (1, 2, 3):
            send(TK.at[:, z], X.at[j, :, rows_of(0)], a_sem, j - 1, y_peer[j])

    def do_j():
        for r in range(8):
            for a in range(2):
                X[0, a, rows_of(PLACE[r])] = TK[a, (z + r) % 8]
        send(X.at[0, :, 0:128], X.at[0, :, 128:256], j_sem, 0, sibling)

    def z_piece(j, place, s, d):
        rows = rows_of(place)
        return X.at[j, :, rows] if s < 3 else X.at[j, "RL".index(d), rows]

    def z_index(j, s, d):
        return ((j - 1) * 4 + s) * 2 + "RL".index(d)

    def z_arrived(j, s, d):
        place = PLACE[7 - s if d == "R" else s + 1]
        arrived(z_piece(j, place, s, d), z_sem, z_index(j, s, d))

    def do_z(j, s, d):
        if s == 0:
            arrived(X.at[j, :, rows_of(0)], a_sem, j - 1)
        else:
            z_arrived(j, s - 1, d)
        place = PLACE[(8 - s) % 8 if d == "R" else s]
        to = PLACE[7 - s if d == "R" else s + 1]
        send(z_piece(j, place, s, d), z_piece(j, to, s, d), z_sem, z_index(j, s, d), ring[d])

    def do_s(j, part):
        for s in STEPS_OF[part]:
            z_arrived(j, s, "R")
            z_arrived(j, s, "L")
        q, n = PLACES_OF[part]
        send(X.at[j, :, rows_of(q, n)], X.at[j, :, rows_of(8 + q, n)], c_sem, (j - 1) * 2 + part, sibling)

    def do_c(j):
        if j == 0:
            arrived(X.at[0, :, 128:256], j_sem, 0)
        else:
            for part, (q, n) in enumerate(PLACES_OF):
                arrived(X.at[j, :, rows_of(8 + q, n)], c_sem, (j - 1) * 2 + part)
        PS[:, j, 0] = times(X[j, 0], WI[...]).astype(BF16).reshape(4, 64, 384)
        PS[:, j, 1] = times_transposed(X[j, 1], WO[...]).astype(BF16).reshape(4, 64, 384)
        for m in (2, 1, 3):
            send(PS.at[x_at[m], j], PR.at[m - 1, j], p_sem, j * 3 + m - 1, x_peer[m])

    def do_d(j):
        total = PS[x, j].astype(F32)
        for m in (1, 2, 3):
            arrived(PR.at[m - 1, j], p_sem, j * 3 + m - 1)
            total = total + PR[m - 1, j].astype(F32)
        YS[j] = total.astype(BF16)
        send(YS.at[j], YR.at[j], y_sem, j, across)

    def do_e(j):
        arrived(YR.at[j], y_sem, j)
        pre, grad = (YS[j, a].astype(F32) + YR[j, a].astype(F32) for a in (0, 1))
        value, slope = gelu_both(pre, grad)
        HC[j, 0, x] = value.astype(BF16)
        HC[j, 1, x] = slope.astype(BF16)
        for m in (2, 1, 3):
            send(HC.at[j, :, x], HC.at[j, :, x], h_sem, j * 4 + m, x_peer[m])

    def do_f(j):
        for m in (1, 2, 3):
            arrived(HC.at[j, :, x_at[4 - m]], h_sem, j * 4 + m)
        for a in (0, 1):
            lhs = HC[j, a].reshape(256, 384)
            val = times(lhs, WO[...]) if a == 0 else times_transposed(lhs, WI[...])
            OP[j, a] = val[0:128]
            SS[j, a] = val[128:256].astype(BF16)
        for part, (q, n) in enumerate(((5, 3), (0, 5))):
            send(SS.at[j, :, rows_of(q, n)], SR.at[j, :, rows_of(q, n)], s_sem, j * 2 + part, sibling)
        HT[:, j * 256:(j + 1) * 256] = HC[j, 0].reshape(256, 384).T
        GT[:, j * 256:(j + 1) * 256] = HC[j, 1].reshape(256, 384).T

    def r_index(j, i, d):
        return (j * 4 + i) * 2 + "RL".index(d)

    def r_ref(buffer, j, i, d):
        direction = "RL".index(d)
        if i == 0:
            return buffer.at[j, i, direction, direction]
        return buffer.at[j, i, direction]

    def both_cores(j, r, a):
        rows = rows_of(PLACE[r])
        return OP[j, a, rows] + SR[j, a, rows].astype(F32)

    def received(j, i, d, a):
        return ZR[j, i, "RL".index(d), a].astype(F32)

    def do_r(j, i, d):
        direction = "RL".index(d)
        q, n = ((5, 3), (0, 5))[i // 2]
        arrived(SR.at[j, :, rows_of(q, n)], s_sem, j * 2 + i // 2)
        r = 4 - i if d == "R" else 4 + i
        if i:
            arrived(r_ref(ZR, j, i - 1, d), r_sem, r_index(j, i - 1, d))
        for a in (0, 1) if i else (direction,):
            total = both_cores(j, r, a)
            if i > 1 or (i == 1 and a == direction):
                total = total + received(j, i - 1, d, a)
            ZS[j, i, direction, a] = total.astype(BF16)
        send(r_ref(ZS, j, i, d), r_ref(ZR, j, i, d), r_sem, r_index(j, i, d), ring[d])

    def do_h(j):
        arrived(SR.at[j, :, rows_of(0, 5)], s_sem, j * 2 + 1)
        for d in "RL":
            arrived(r_ref(ZR, j, 3, d), r_sem, r_index(j, 3, d))
        for a in (0, 1):
            total = both_cores(j, 0, a) + received(j, 3, "R", a) + received(j, 3, "L", a)
            if j == 0:
                FO[a] = total
            else:
                FS[j - 1, a] = total.astype(BF16)
        if j:
            send(FS.at[j - 1], FR.at[j - 1], f_sem, j - 1, y_peer[j])

    def do_w(k):
        cols = pl.ds(k * 256, min(256, 1152 - k * 256))
        GI[cols, :] = times(GT[...], X[:, 0, :, cols].reshape(1024, cols.size)).T.astype(BF16)
        GO[:, cols] = times(HT[...], X[:, 1, :, cols].reshape(1024, cols.size)).astype(BF16)

    def do_fin():
        stores = [
            pltpu.make_async_copy(GI, grad_weight_in, local_sem.at[4]),
            pltpu.make_async_copy(GO, grad_weight_out, local_sem.at[5]),
        ]
        for copy in stores:
            copy.start()
        total = FO[...]
        for j in (1, 2, 3):
            arrived(FR.at[j - 1], f_sem, j - 1)
            total = total + FR[j - 1].astype(F32)
        OB[...] = total.astype(BF16)
        stores.append(pltpu.make_async_copy(OB.at[0], layer_out, local_sem.at[6]))
        stores.append(pltpu.make_async_copy(OB.at[1], grad_tokens, local_sem.at[7]))
        stores[2].start()
        stores[3].start()
        for copy in pending:
            copy.wait_send()
        for copy in stores:
            copy.wait()

    steps = {
        "A": do_a, "J": do_j, "Z": do_z, "S": do_s, "C": do_c, "D": do_d, "E": do_e, "F": do_f,
        "R": do_r, "H": do_h, "W": do_w, "FIN": do_fin,
    }
    weights_here = False
    for step in ORDER:
        if step[0] == "C" and not weights_here:
            fetch[2].wait()
            fetch[3].wait()
            weights_here = True
        steps[step[0]](*step[1:])
        while len(pending) > 24:
            pending.pop(0).wait_send()


def hand_out(*refs):
    results, outputs, held, arrive, leave = refs[0:4], refs[4:8], refs[8:12], refs[12], refs[13]
    order = (2, 3, 0, 1)
    fetches = {i: pltpu.make_async_copy(results[i], held[i], arrive.at[i]) for i in order}
    stores = {i: pltpu.make_async_copy(held[i], outputs[i], leave.at[i]) for i in order}
    for i in order:
        fetches[i].start()
    for i in order:
        fetches[i].wait()
        stores[i].start()
    for i in order:
        stores[i].wait()


def shards(tokens, weight_in, weight_out, grad_out):
    any_space = pl.BlockSpec(memory_space=pl.ANY)
    dma = pltpu.SemaphoreType.DMA
    shapes = (
        jax.ShapeDtypeStruct((16, 1152), BF16),
        jax.ShapeDtypeStruct((16, 1152), BF16),
        jax.ShapeDtypeStruct((1152, 384), BF16),
        jax.ShapeDtypeStruct((384, 1152), BF16),
    )
    results = pl.pallas_call(
        kernel,
        out_shape=shapes,
        in_specs=[any_space] * 4,
        out_specs=(any_space,) * 4,
        scratch_shapes=[
            pltpu.VMEM((2, 8, 16, 1152), BF16),
            pltpu.VMEM((4, 2, 256, 1152), BF16),
            pltpu.VMEM((1152, 384), BF16),
            pltpu.VMEM((384, 1152), BF16),
            pltpu.VMEM((4, 4, 2, 64, 384), BF16),
            pltpu.VMEM((3, 4, 2, 64, 384), BF16),
            pltpu.VMEM((4, 2, 64, 384), BF16),
            pltpu.VMEM((4, 2, 64, 384), BF16),
            pltpu.VMEM((4, 2, 4, 64, 384), BF16),
            pltpu.VMEM((384, 1024), BF16),
            pltpu.VMEM((384, 1024), BF16),
            pltpu.VMEM((4, 2, 128, 1152), BF16),
            pltpu.VMEM((4, 2, 128, 1152), BF16),
            pltpu.VMEM((4, 2, 128, 1152), F32),
            pltpu.VMEM((4, 4, 2, 2, 16, 1152), BF16),
            pltpu.VMEM((4, 4, 2, 2, 16, 1152), BF16),
            pltpu.VMEM((3, 2, 16, 1152), BF16),
            pltpu.VMEM((3, 2, 16, 1152), BF16),
            pltpu.VMEM((2, 16, 1152), F32),
            pltpu.VMEM((2, 16, 1152), BF16),
            pltpu.VMEM((1152, 384), BF16),
            pltpu.VMEM((384, 1152), BF16),
            dma((8,)),
            dma((3,)), dma((3,)),
            dma((1,)), dma((1,)),
            dma((6,)), dma((6,)),
            dma((24,)), dma((24,)),
            dma((12,)), dma((12,)),
            dma((4,)), dma((4,)),
            dma((16,)), dma((16,)),
            dma((8,)), dma((8,)),
            dma((32,)), dma((32,)),
            dma((3,)), dma((3,)),
        ],
        compiler_params=pltpu.CompilerParams(
            collective_id=0, has_side_effects=True, vmem_limit_bytes=56 * 1024 * 1024
        ),
        cost_estimate=pl.CostEstimate(flops=5436000000, bytes_accessed=8000000, transcendentals=1000000),
    )(tokens.reshape(8, 16, 1152), weight_in, weight_out, grad_out.reshape(8, 16, 1152))
    return pl.pallas_call(
        hand_out,
        out_shape=shapes,
        in_specs=[any_space] * 4,
        out_specs=(any_space,) * 4,
        scratch_shapes=[*(pltpu.VMEM(shape.shape, BF16) for shape in shapes), dma((4,)), dma((4,))],
    )(*results)


def solution(mesh):
    placed = (P("dp", "row"), P("row", ("dp", "col")), P(("dp", "col"), "row"), P("dp", "row"))
    return jax.shard_map(
        shards,
        mesh=mesh,
        in_specs=placed,
        out_specs=(
            P(("dp", "col"), "row"),
            P(("dp", "col"), "row"),
            P("row", ("dp", "col")),
            P(("dp", "col"), "row"),
        ),
        check_vma=False,
    )
```

```python
import jax
import jax.numpy as jnp
from jax import lax
from jax.experimental import pallas as pl
from jax.experimental.pallas import tpu as pltpu
from jax.sharding import PartitionSpec as P

MESH = pl.DeviceIdType.MESH
BF16 = jnp.bfloat16
F32 = jnp.float32

PLACE = {0: 0, 1: 1, 7: 2, 2: 3, 6: 4, 3: 5, 5: 6, 4: 7}
STEPS_OF = ((0, 1), (2, 3))
PLACES_OF = ((0, 5), (5, 3))

ORDER = (
    ("A",), ("J",), ("Z", 1, 0, "R"), ("Z", 1, 0, "L"), ("Z", 2, 0, "R"), ("Z", 2, 0, "L"), ("Z", 1, 1, "R"),
    ("Z", 1, 1, "L"), ("C", 0), ("Z", 3, 0, "R"), ("Z", 3, 0, "L"), ("Z", 2, 1, "R"), ("Z", 2, 1, "L"),
    ("Z", 1, 2, "R"), ("S", 1, 0), ("Z", 1, 2, "L"), ("Z", 3, 1, "R"), ("Z", 3, 1, "L"), ("Z", 2, 2, "R"),
    ("S", 2, 0), ("Z", 2, 2, "L"), ("Z", 1, 3, "R"), ("Z", 1, 3, "L"), ("D", 0), ("Z", 3, 2, "R"), ("S", 3, 0),
    ("Z", 3, 2, "L"), ("Z", 2, 3, "R"), ("Z", 2, 3, "L"), ("S", 1, 1), ("Z", 3, 3, "R"), ("Z", 3, 3, "L"),
    ("S", 2, 1), ("S", 3, 1), ("C", 1), ("C", 2), ("C", 3), ("E", 0), ("D", 1), ("D", 2), ("E", 1), ("D", 3),
    ("F", 0), ("E", 2), ("F", 1), ("R", 0, 0, "R"), ("E", 3), ("R", 0, 0, "L"), ("R", 0, 1, "R"), ("F", 2),
    ("R", 0, 1, "L"), ("R", 1, 0, "R"), ("R", 0, 2, "R"), ("R", 1, 0, "L"), ("R", 1, 1, "R"), ("R", 0, 2, "L"),
    ("F", 3), ("R", 2, 0, "R"), ("R", 0, 3, "R"), ("R", 2, 0, "L"), ("R", 0, 3, "L"), ("R", 1, 1, "L"),
    ("R", 1, 2, "R"), ("W", 0), ("R", 2, 1, "R"), ("R", 2, 1, "L"), ("W", 1), ("R", 3, 0, "R"), ("H", 0),
    ("R", 1, 3, "R"), ("R", 1, 2, "L"), ("R", 3, 0, "L"), ("R", 2, 2, "R"), ("W", 2), ("R", 3, 1, "R"),
    ("R", 2, 2, "L"), ("W", 3), ("R", 3, 1, "L"), ("R", 2, 3, "R"), ("R", 1, 3, "L"), ("W", 4), ("R", 3, 2, "R"),
    ("R", 2, 3, "L"), ("R", 3, 2, "L"), ("H", 1), ("R", 3, 3, "R"), ("H", 2), ("R", 3, 3, "L"), ("H", 3), ("FIN",),
)


def gelu_both(pre_value, grad_value):
    square = pre_value * pre_value
    tanh_part = jnp.tanh(0.7978845608 * (pre_value + 0.044715 * square * pre_value))
    inner_slope = 0.7978845608 * (1.0 + 0.134145 * square)
    value = 0.5 * pre_value * (1.0 + tanh_part)
    slope = 0.5 * (1.0 + tanh_part) + 0.5 * pre_value * (1.0 - tanh_part * tanh_part) * inner_slope
    return value, grad_value * slope


def rows_of(place, count=1):
    return pl.ds(place * 16, count * 16)


def times(left, right):
    return jnp.dot(left, right, preferred_element_type=F32)


def times_transposed(left, right):
    return lax.dot_general(left, right, (((1,), (1,)), ((), ())), preferred_element_type=F32)


def kernel(
    tokens, weight_in, weight_out, grad_out,
    layer_out, grad_tokens, grad_weight_in, grad_weight_out,
    TK, X, WI, WO, PS, PR, YS, YR, HC, HT, GT, SS, SR, OP, ZS, ZR, FS, FR, FO, OB, GI, GO,
    local_sem, a_send, a_recv, j_send, j_recv, c_send, c_recv, z_send, z_recv,
    p_send, p_recv, y_send, y_recv, h_send, h_recv, s_send, s_recv, r_send, r_recv, f_send, f_recv,
):
    dp = lax.axis_index("dp")
    row = lax.axis_index("row")
    z = lax.axis_index("col")
    y, core = dp // 2, dp % 2
    half, x = row // 4, row % 4

    def device(y=y, core=core, half=half, x=x, z=z):
        return {"dp": y * 2 + core, "row": half * 4 + x, "col": z}

    sibling = device(core=1 - core)
    ring = {"R": device(z=(z + 1) % 8), "L": device(z=(z + 7) % 8)}
    across = device(half=1 - half)
    y_peer = {1: device(y=y + 1 - 2 * (y % 2)), 2: device(y=(y + 2) % 4), 3: device(y=3 - y)}
    x_at = {m: (x + m) % 4 for m in (1, 2, 3)}
    x_peer = {m: device(x=x_at[m]) for m in (1, 2, 3)}

    waited = set()

    def send(src, dst, sems, index, to):
        copy = pltpu.make_async_remote_copy(
            src_ref=src, dst_ref=dst, send_sem=sems[0], recv_sem=sems[1].at[index],
            device_id=to, device_id_type=MESH,
        )
        copy.start()

    def arrived(dst, sems, index):
        if (id(sems), index) in waited:
            return
        waited.add((id(sems), index))
        pltpu.make_async_remote_copy(
            src_ref=dst, dst_ref=dst, send_sem=sems[0], recv_sem=sems[1].at[index],
            device_id=sibling, device_id_type=MESH,
        ).wait_recv()

    def all_left(ref, sems):
        pltpu.make_async_remote_copy(
            src_ref=ref, dst_ref=ref, send_sem=sems[0], recv_sem=sems[1].at[0],
            device_id=sibling, device_id_type=MESH,
        ).wait_send()

    a_sem, j_sem, c_sem, z_sem = (a_send, a_recv), (j_send, j_recv), (c_send, c_recv), (z_send, z_recv)
    p_sem, y_sem, h_sem, s_sem = (p_send, p_recv), (y_send, y_recv), (h_send, h_recv), (s_send, s_recv)
    r_sem, f_sem = (r_send, r_recv), (f_send, f_recv)

    barrier = pltpu.get_barrier_semaphore()
    peers = [sibling, *ring.values(), *y_peer.values(), *x_peer.values()]
    peers += [across]
    for peer in peers:
        pl.semaphore_signal(barrier, inc=1, device_id=peer, device_id_type=MESH)
    fetch = [
        pltpu.make_async_copy(tokens, TK.at[0], local_sem.at[0]),
        pltpu.make_async_copy(grad_out, TK.at[1], local_sem.at[1]),
        pltpu.make_async_copy(weight_in, WI, local_sem.at[2]),
        pltpu.make_async_copy(weight_out, WO, local_sem.at[3]),
    ]
    for copy in fetch:
        copy.start()

    pl.semaphore_wait(barrier, len(peers))
    fetch[0].wait()
    fetch[1].wait()

    def do_a():
        for j in (1, 2, 3):
            send(TK.at[:, z], X.at[j, :, rows_of(0)], a_sem, j - 1, y_peer[j])

    def do_j():
        for r in range(8):
            for a in range(2):
                X[0, a, rows_of(PLACE[r])] = TK[a, (z + r) % 8]
        send(X.at[0, :, 0:128], X.at[0, :, 128:256], j_sem, 0, sibling)

    def z_piece(j, place, s, d):
        rows = rows_of(place)
        return X.at[j, :, rows] if s < 3 else X.at[j, "RL".index(d), rows]

    def z_index(j, s, d):
        return ((j - 1) * 4 + s) * 2 + "RL".index(d)

    def z_arrived(j, s, d):
        place = PLACE[7 - s if d == "R" else s + 1]
        arrived(z_piece(j, place, s, d), z_sem, z_index(j, s, d))

    def do_z(j, s, d):
        if s == 0:
            arrived(X.at[j, :, rows_of(0)], a_sem, j - 1)
        else:
            z_arrived(j, s - 1, d)
        place = PLACE[(8 - s) % 8 if d == "R" else s]
        to = PLACE[7 - s if d == "R" else s + 1]
        send(z_piece(j, place, s, d), z_piece(j, to, s, d), z_sem, z_index(j, s, d), ring[d])

    def do_s(j, part):
        for s in STEPS_OF[part]:
            z_arrived(j, s, "R")
            z_arrived(j, s, "L")
        q, n = PLACES_OF[part]
        send(X.at[j, :, rows_of(q, n)], X.at[j, :, rows_of(8 + q, n)], c_sem, j - 1, sibling)

    def do_c(j):
        if j == 0:
            arrived(X.at[0, :, 128:256], j_sem, 0)
        else:
            arrived(X.at[j, :, 128:256], c_sem, j - 1)
        PS[:, j, 0] = times(X[j, 0], WI[...]).astype(BF16).reshape(4, 64, 384)
        PS[:, j, 1] = times_transposed(X[j, 1], WO[...]).astype(BF16).reshape(4, 64, 384)
        for m in (2, 1, 3):
            send(PS.at[x_at[m], j], PR.at[m - 1, j], p_sem, j, x_peer[m])

    def do_d(j):
        arrived(PR.at[:, j], p_sem, j)
        total = PS[x, j].astype(F32)
        for m in (1, 2, 3):
            total = total + PR[m - 1, j].astype(F32)
        YS[j] = total.astype(BF16)
        send(YS.at[j], YR.at[j], y_sem, j, across)

    def do_e(j):
        arrived(YR.at[j], y_sem, j)
        pre, grad = (YS[j, a].astype(F32) + YR[j, a].astype(F32) for a in (0, 1))
        value, slope = gelu_both(pre, grad)
        HC[j, 0, x] = value.astype(BF16)
        HC[j, 1, x] = slope.astype(BF16)
        for m in (2, 1, 3):
            send(HC.at[j, :, x], HC.at[j, :, x], h_sem, j, x_peer[m])

    def do_f(j):
        arrived(PR.at[:, j], h_sem, j)
        for a in (0, 1):
            lhs = HC[j, a].reshape(256, 384)
            val = times(lhs, WO[...]) if a == 0 else times_transposed(lhs, WI[...])
            OP[j, a] = val[0:128]
            SS[j, a] = val[128:256].astype(BF16)
            send(SS.at[j, a], SR.at[j, a], s_sem, j * 2 + a, sibling)
        HT[:, j * 256:(j + 1) * 256] = HC[j, 0].reshape(256, 384).T
        GT[:, j * 256:(j + 1) * 256] = HC[j, 1].reshape(256, 384).T

    def r_index(j, i, d):
        return (j * 4 + i) * 2 + "RL".index(d)

    def r_ref(buffer, j, i, d):
        direction = "RL".index(d)
        if i == 0:
            return buffer.at[j, i, direction, direction]
        return buffer.at[j, i, direction]

    def both_cores(j, r, a):
        rows = rows_of(PLACE[r])
        return OP[j, a, rows] + SR[j, a, rows].astype(F32)

    def received(j, i, d, a):
        return ZR[j, i, "RL".index(d), a].astype(F32)

    def do_r(j, i, d):
        direction = "RL".index(d)
        for a in (0, 1) if i else (direction,):
            arrived(SR.at[j, a], s_sem, j * 2 + a)
        r = 4 - i if d == "R" else 4 + i
        if i:
            arrived(r_ref(ZR, j, i - 1, d), r_sem, r_index(j, i - 1, d))
        for a in (0, 1) if i else (direction,):
            total = both_cores(j, r, a)
            if i > 1 or (i == 1 and a == direction):
                total = total + received(j, i - 1, d, a)
            ZS[j, i, direction, a] = total.astype(BF16)
        send(r_ref(ZS, j, i, d), r_ref(ZR, j, i, d), r_sem, r_index(j, i, d), ring[d])

    def do_h(j):
        for a in (0, 1):
            arrived(SR.at[j, a], s_sem, j * 2 + a)
        for d in "RL":
            arrived(r_ref(ZR, j, 3, d), r_sem, r_index(j, 3, d))
        for a in (0, 1):
            total = both_cores(j, 0, a) + received(j, 3, "R", a) + received(j, 3, "L", a)
            if j == 0:
                FO[a] = total
            else:
                FS[j - 1, a] = total.astype(BF16)
        if j:
            send(FS.at[j - 1], FR.at[j - 1], f_sem, j - 1, y_peer[j])

    def do_w(k):
        cols = pl.ds(k * 256, min(256, 1152 - k * 256))
        GI[cols, :] = times(GT[...], X[:, 0, :, cols].reshape(1024, cols.size)).T.astype(BF16)
        GO[:, cols] = times(HT[...], X[:, 1, :, cols].reshape(1024, cols.size)).astype(BF16)

    def do_fin():
        stores = [
            pltpu.make_async_copy(GI, grad_weight_in, local_sem.at[4]),
            pltpu.make_async_copy(GO, grad_weight_out, local_sem.at[5]),
        ]
        for copy in stores:
            copy.start()
        total = FO[...]
        for j in (1, 2, 3):
            arrived(FR.at[j - 1], f_sem, j - 1)
            total = total + FR[j - 1].astype(F32)
        OB[...] = total.astype(BF16)
        stores.append(pltpu.make_async_copy(OB.at[0], layer_out, local_sem.at[6]))
        stores.append(pltpu.make_async_copy(OB.at[1], grad_tokens, local_sem.at[7]))
        stores[2].start()
        stores[3].start()
        all_left(FS, a_sem)
        all_left(X.at[0, :, 0:128], j_sem)
        all_left(X.at[1:4, :, 0:128], c_sem)
        all_left(X.at[1:4, :, 0:112], z_sem)
        all_left(PR, p_sem)
        all_left(YS, y_sem)
        all_left(PR, h_sem)
        all_left(SS, s_sem)
        all_left(X.at[:, :, 0:112], r_sem)
        all_left(FS, f_sem)
        for copy in stores:
            copy.wait()

    steps = {
        "A": do_a, "J": do_j, "Z": do_z, "S": do_s, "C": do_c, "D": do_d, "E": do_e, "F": do_f,
        "R": do_r, "H": do_h, "W": do_w, "FIN": do_fin,
    }
    weights_here = False
    for step in ORDER:
        if step[0] == "C" and not weights_here:
            fetch[2].wait()
            fetch[3].wait()
            weights_here = True
        steps[step[0]](*step[1:])


def hand_out(*refs):
    results, outputs, held, arrive, leave = refs[0:4], refs[4:8], refs[8:12], refs[12], refs[13]
    order = (2, 3, 0, 1)
    fetches = {i: pltpu.make_async_copy(results[i], held[i], arrive.at[i]) for i in order}
    stores = {i: pltpu.make_async_copy(held[i], outputs[i], leave.at[i]) for i in order}
    for i in order:
        fetches[i].start()
    for i in order:
        fetches[i].wait()
        stores[i].start()
    for i in order:
        stores[i].wait()


def shards(tokens, weight_in, weight_out, grad_out):
    any_space = pl.BlockSpec(memory_space=pl.ANY)
    dma = pltpu.SemaphoreType.DMA
    shapes = (
        jax.ShapeDtypeStruct((16, 1152), BF16),
        jax.ShapeDtypeStruct((16, 1152), BF16),
        jax.ShapeDtypeStruct((1152, 384), BF16),
        jax.ShapeDtypeStruct((384, 1152), BF16),
    )
    results = pl.pallas_call(
        kernel,
        out_shape=shapes,
        in_specs=[any_space] * 4,
        out_specs=(any_space,) * 4,
        scratch_shapes=[
            pltpu.VMEM((2, 8, 16, 1152), BF16),
            pltpu.VMEM((4, 2, 256, 1152), BF16),
            pltpu.VMEM((1152, 384), BF16),
            pltpu.VMEM((384, 1152), BF16),
            pltpu.VMEM((4, 4, 2, 64, 384), BF16),
            pltpu.VMEM((3, 4, 2, 64, 384), BF16),
            pltpu.VMEM((4, 2, 64, 384), BF16),
            pltpu.VMEM((4, 2, 64, 384), BF16),
            pltpu.VMEM((4, 2, 4, 64, 384), BF16),
            pltpu.VMEM((384, 1024), BF16),
            pltpu.VMEM((384, 1024), BF16),
            pltpu.VMEM((4, 2, 128, 1152), BF16),
            pltpu.VMEM((4, 2, 128, 1152), BF16),
            pltpu.VMEM((4, 2, 128, 1152), F32),
            pltpu.VMEM((4, 4, 2, 2, 16, 1152), BF16),
            pltpu.VMEM((4, 4, 2, 2, 16, 1152), BF16),
            pltpu.VMEM((3, 2, 16, 1152), BF16),
            pltpu.VMEM((3, 2, 16, 1152), BF16),
            pltpu.VMEM((2, 16, 1152), F32),
            pltpu.VMEM((2, 16, 1152), BF16),
            pltpu.VMEM((1152, 384), BF16),
            pltpu.VMEM((384, 1152), BF16),
            dma((8,)),
            dma, dma((3,)),
            dma, dma((1,)),
            dma, dma((3,)),
            dma, dma((24,)),
            dma, dma((4,)),
            dma, dma((4,)),
            dma, dma((4,)),
            dma, dma((8,)),
            dma, dma((32,)),
            dma, dma((3,)),
        ],
        compiler_params=pltpu.CompilerParams(
            collective_id=0, has_side_effects=True, vmem_limit_bytes=56 * 1024 * 1024
        ),
        cost_estimate=pl.CostEstimate(flops=5436000000, bytes_accessed=8000000, transcendentals=1000000),
    )(tokens.reshape(8, 16, 1152), weight_in, weight_out, grad_out.reshape(8, 16, 1152))
    return pl.pallas_call(
        hand_out,
        out_shape=shapes,
        in_specs=[any_space] * 4,
        out_specs=(any_space,) * 4,
        scratch_shapes=[*(pltpu.VMEM(shape.shape, BF16) for shape in shapes), dma((4,)), dma((4,))],
    )(*results)


def solution(mesh):
    placed = (P("dp", "row"), P("row", ("dp", "col")), P(("dp", "col"), "row"), P("dp", "row"))
    return jax.shard_map(
        shards,
        mesh=mesh,
        in_specs=placed,
        out_specs=(
            P(("dp", "col"), "row"),
            P(("dp", "col"), "row"),
            P("row", ("dp", "col")),
            P(("dp", "col"), "row"),
        ),
        check_vma=False,
    )
```

```python
import jax
import jax.numpy as jnp
from jax import lax
from jax.experimental import pallas as pl
from jax.experimental.pallas import tpu as pltpu
from jax.sharding import PartitionSpec as P

MESH = pl.DeviceIdType.MESH
BF16 = jnp.bfloat16
F32 = jnp.float32

PLACE = {0: 0, 4: 1, 7: 2, 3: 3, 1: 4, 5: 5, 2: 6, 6: 7}
ORDER = (
    ("A",), ("J",), ("Z", 1, 0, "R"), ("Z", 1, 0, "L"), ("C", 0), ("Z", 1, 1, "R"), ("Z", 1, 1, "L"), ("S", 1, 0),
    ("Z", 2, 0, "R"), ("Z", 2, 0, "L"), ("S", 1, 1), ("D", 0), ("C", 1), ("Z", 2, 1, "R"), ("Z", 2, 1, "L"),
    ("Z", 3, 0, "L"), ("Z", 3, 0, "R"), ("S", 2, 0), ("E", 0), ("S", 2, 1), ("D", 1), ("Z", 3, 1, "R"),
    ("Z", 3, 1, "L"), ("S", 3, 0), ("C", 2), ("S", 3, 1), ("F", 0), ("C", 3), ("D", 2), ("R", 0, 0, "R"),
    ("R", 0, 0, "L"), ("E", 1), ("R", 0, 1, "R"), ("D", 3), ("R", 0, 1, "L"), ("E", 2), ("R", 0, 2, "R"), ("F", 1),
    ("R", 0, 2, "L"), ("E", 3), ("F", 2), ("R", 1, 0, "R"), ("R", 1, 0, "L"), ("R", 2, 0, "R"), ("R", 1, 1, "R"),
    ("R", 2, 0, "L"), ("R", 1, 1, "L"), ("F", 3), ("R", 2, 1, "R"), ("R", 2, 1, "L"), ("R", 1, 2, "R"),
    ("R", 1, 2, "L"), ("R", 3, 0, "R"), ("R", 3, 0, "L"), ("R", 2, 2, "R"), ("R", 2, 2, "L"), ("R", 3, 1, "R"),
    ("R", 3, 1, "L"), ("W", 2), ("R", 2, 3, "R"), ("R", 2, 3, "L"), ("R", 3, 2, "R"), ("R", 3, 2, "L"),
    ("R", 1, 3, "L"), ("R", 1, 3, "R"), ("H", 2), ("R", 3, 3, "R"), ("R", 3, 3, "L"), ("R", 0, 3, "L"),
    ("R", 0, 3, "R"), ("H", 1), ("W", 4), ("H", 3), ("W", 1), ("W", 0), ("H", 0), ("W", 3), ("FIN",),
)


def gelu_both(pre_value, grad_value):
    square = pre_value * pre_value
    tanh_part = jnp.tanh(0.7978845608 * (pre_value + 0.044715 * square * pre_value))
    inner_slope = 0.7978845608 * (1.0 + 0.134145 * square)
    value = 0.5 * pre_value * (1.0 + tanh_part)
    slope = 0.5 * (1.0 + tanh_part) + 0.5 * pre_value * (1.0 - tanh_part * tanh_part) * inner_slope
    return value, grad_value * slope


def rows_of(place, count=1):
    return pl.ds(place * 16, count * 16)


def times(left, right):
    return jnp.dot(left, right, preferred_element_type=F32)


def times_transposed(left, right):
    return lax.dot_general(left, right, (((1,), (1,)), ((), ())), preferred_element_type=F32)


def kernel(
    tokens, weight_in, weight_out, grad_out,
    layer_out, grad_tokens, grad_weight_in, grad_weight_out,
    TK, X, WI, WO, PS, PR, YS, YR, HC, HT, GT, SS, SR, OP, ZS, ZR, FS, FR, FO, OB, GI, GO,
    local_sem, a_send, a_recv, j_send, j_recv, c_send, c_recv, z_send, z_recv,
    p_send, p_recv, y_send, y_recv, h_send, h_recv, s_send, s_recv, r_send, r_recv, f_send, f_recv,
):
    dp = lax.axis_index("dp")
    row = lax.axis_index("row")
    z = lax.axis_index("col")
    y, core = dp // 2, dp % 2
    half, x = row // 4, row % 4

    def device(y=y, core=core, half=half, x=x, z=z):
        return {"dp": y * 2 + core, "row": half * 4 + x, "col": z}

    sibling = device(core=1 - core)
    ring = {"R": device(z=(z + 1) % 8), "L": device(z=(z + 7) % 8)}
    across = device(half=1 - half)
    y_peer = {1: device(y=y + 1 - 2 * (y % 2)), 2: device(y=(y + 2) % 4), 3: device(y=3 - y)}
    x_at = {m: (x + m) % 4 for m in (1, 2, 3)}
    x_peer = {m: device(x=x_at[m]) for m in (1, 2, 3)}

    waited = set()

    def send(src, dst, sems, index, to):
        copy = pltpu.make_async_remote_copy(
            src_ref=src, dst_ref=dst, send_sem=sems[0], recv_sem=sems[1].at[index],
            device_id=to, device_id_type=MESH,
        )
        copy.start()

    def arrived(dst, sems, index):
        if (id(sems), index) in waited:
            return
        waited.add((id(sems), index))
        pltpu.make_async_remote_copy(
            src_ref=dst, dst_ref=dst, send_sem=sems[0], recv_sem=sems[1].at[index],
            device_id=sibling, device_id_type=MESH,
        ).wait_recv()

    def all_left(ref, sems):
        pltpu.make_async_remote_copy(
            src_ref=ref, dst_ref=ref, send_sem=sems[0], recv_sem=sems[1].at[0],
            device_id=sibling, device_id_type=MESH,
        ).wait_send()

    a_sem, j_sem, c_sem, z_sem = (a_send, a_recv), (j_send, j_recv), (c_send, c_recv), (z_send, z_recv)
    p_sem, y_sem, h_sem, s_sem = (p_send, p_recv), (y_send, y_recv), (h_send, h_recv), (s_send, s_recv)
    r_sem, f_sem = (r_send, r_recv), (f_send, f_recv)

    barrier = pltpu.get_barrier_semaphore()
    peers = [sibling, *ring.values(), *y_peer.values(), *x_peer.values()]
    peers += [across]
    for peer in peers:
        pl.semaphore_signal(barrier, inc=1, device_id=peer, device_id_type=MESH)
    fetch = [
        pltpu.make_async_copy(tokens, TK.at[0], local_sem.at[0]),
        pltpu.make_async_copy(grad_out, TK.at[1], local_sem.at[1]),
        pltpu.make_async_copy(weight_in, WI, local_sem.at[2]),
        pltpu.make_async_copy(weight_out, WO, local_sem.at[3]),
    ]
    for copy in fetch:
        copy.start()

    pl.semaphore_wait(barrier, len(peers))
    fetch[0].wait()
    fetch[1].wait()

    def fill(distances):
        for r in distances:
            for a in range(2):
                X[0, a, rows_of(PLACE[r])] = TK[a, (z + r) % 8]

    def do_a():
        fill((0, 4))
        for j in (1, 2, 3):
            send(X.at[0, :, rows_of(0, 2)], X.at[j, :, rows_of(0, 2)], a_sem, j - 1, y_peer[j])

    def do_j():
        fill((1, 2, 3, 5, 6, 7))
        send(X.at[0, :, 0:128], X.at[0, :, 128:256], j_sem, 0, sibling)

    def z_rows(s, d):
        return rows_of(2 if d == "R" else 4, 2) if s == 0 else rows_of(7 if d == "R" else 6)

    def z_arrived(j, s, d):
        arrived(X.at[j, :, z_rows(s, d)], z_sem, ((j - 1) * 2 + s) * 2 + "RL".index(d))

    def do_z(j, s, d):
        if s == 0:
            arrived(X.at[j, :, rows_of(0, 2)], a_sem, j - 1)
            source = rows_of(0, 2)
        else:
            z_arrived(j, 0, d)
            source = rows_of(2 if d == "R" else 4)
        index = ((j - 1) * 2 + s) * 2 + "RL".index(d)
        send(X.at[j, :, source], X.at[j, :, z_rows(s, d)], z_sem, index, ring[d])

    def do_s(j, part):
        if part == 0:
            arrived(X.at[j, :, rows_of(0, 2)], a_sem, j - 1)
        for d in "RL":
            z_arrived(j, part, d)
        q, n = ((0, 6), (6, 2))[part]
        send(X.at[j, :, rows_of(q, n)], X.at[j, :, rows_of(8 + q, n)], c_sem, j - 1, sibling)

    def do_c(j):
        if j == 0:
            arrived(X.at[0, :, 128:256], j_sem, 0)
        else:
            arrived(X.at[j, :, 128:256], c_sem, j - 1)
        PS[:, j, 0] = times(X[j, 0], WI[...]).astype(BF16).reshape(4, 64, 384)
        PS[:, j, 1] = times_transposed(X[j, 1], WO[...]).astype(BF16).reshape(4, 64, 384)
        for m in (2, 1, 3):
            send(PS.at[x_at[m], j], PR.at[m - 1, j], p_sem, j, x_peer[m])

    def do_d(j):
        arrived(PR.at[:, j], p_sem, j)
        total = PS[x, j].astype(F32)
        for m in (1, 2, 3):
            total = total + PR[m - 1, j].astype(F32)
        YS[j] = total.astype(BF16)
        send(YS.at[j], YR.at[j], y_sem, j, across)

    def do_e(j):
        arrived(YR.at[j], y_sem, j)
        pre, grad = (YS[j, a].astype(F32) + YR[j, a].astype(F32) for a in (0, 1))
        value, slope = gelu_both(pre, grad)
        HC[j, 0, x] = value.astype(BF16)
        HC[j, 1, x] = slope.astype(BF16)
        for m in (2, 1, 3):
            send(HC.at[j, :, x], HC.at[j, :, x], h_sem, j, x_peer[m])

    def do_f(j):
        arrived(PR.at[:, j], h_sem, j)
        for a in (0, 1):
            lhs = HC[j, a].reshape(256, 384)
            val = times(lhs, WO[...]) if a == 0 else times_transposed(lhs, WI[...])
            OP[j, a] = val[0:128]
            SS[j, a] = val[128:256].astype(BF16)
            send(SS.at[j, a], SR.at[j, a], s_sem, j * 2 + a, sibling)
        HT[:, j * 256:(j + 1) * 256] = HC[j, 0].reshape(256, 384).T
        GT[:, j * 256:(j + 1) * 256] = HC[j, 1].reshape(256, 384).T

    def r_index(j, i, d):
        return (j * 4 + i) * 2 + "RL".index(d)

    def r_ref(buffer, j, i, d):
        direction = "RL".index(d)
        if i == 0:
            return buffer.at[j, i, direction, direction]
        return buffer.at[j, i, direction]

    def both_cores(j, r, a):
        rows = rows_of(PLACE[r])
        return OP[j, a, rows] + SR[j, a, rows].astype(F32)

    def received(j, i, d, a):
        return ZR[j, i, "RL".index(d), a].astype(F32)

    def do_r(j, i, d):
        direction = "RL".index(d)
        for a in (0, 1) if i else (direction,):
            arrived(SR.at[j, a], s_sem, j * 2 + a)
        r = 4 - i if d == "R" else 4 + i
        if i:
            arrived(r_ref(ZR, j, i - 1, d), r_sem, r_index(j, i - 1, d))
        for a in (0, 1) if i else (direction,):
            total = both_cores(j, r, a)
            if i > 1 or (i == 1 and a == direction):
                total = total + received(j, i - 1, d, a)
            ZS[j, i, direction, a] = total.astype(BF16)
        send(r_ref(ZS, j, i, d), r_ref(ZR, j, i, d), r_sem, r_index(j, i, d), ring[d])

    def do_h(j):
        for a in (0, 1):
            arrived(SR.at[j, a], s_sem, j * 2 + a)
        for d in "RL":
            arrived(r_ref(ZR, j, 3, d), r_sem, r_index(j, 3, d))
        for a in (0, 1):
            total = both_cores(j, 0, a) + received(j, 3, "R", a) + received(j, 3, "L", a)
            if j == 0:
                FO[a] = total
            else:
                FS[j - 1, a] = total.astype(BF16)
        if j:
            send(FS.at[j - 1], FR.at[j - 1], f_sem, j - 1, y_peer[j])

    def do_w(k):
        cols = pl.ds(k * 256, min(256, 1152 - k * 256))
        GI[cols, :] = times(GT[...], X[:, 0, :, cols].reshape(1024, cols.size)).T.astype(BF16)
        GO[:, cols] = times(HT[...], X[:, 1, :, cols].reshape(1024, cols.size)).astype(BF16)

    def do_fin():
        stores = [
            pltpu.make_async_copy(GI, grad_weight_in, local_sem.at[4]),
            pltpu.make_async_copy(GO, grad_weight_out, local_sem.at[5]),
        ]
        for copy in stores:
            copy.start()
        total = FO[...]
        for j in (1, 2, 3):
            arrived(FR.at[j - 1], f_sem, j - 1)
            total = total + FR[j - 1].astype(F32)
        OB[...] = total.astype(BF16)
        stores.append(pltpu.make_async_copy(OB.at[0], layer_out, local_sem.at[6]))
        stores.append(pltpu.make_async_copy(OB.at[1], grad_tokens, local_sem.at[7]))
        stores[2].start()
        stores[3].start()
        all_left(X.at[1:4, :, 0:32], a_sem)
        all_left(X.at[0, :, 0:128], j_sem)
        all_left(X.at[1:4, :, 0:128], c_sem)
        all_left(X.at[1:4, :, 0:96], z_sem)
        all_left(PR, p_sem)
        all_left(YS, y_sem)
        all_left(PR, h_sem)
        all_left(SS, s_sem)
        all_left(X.at[:, :, 0:112], r_sem)
        all_left(FS, f_sem)
        for copy in stores:
            copy.wait()

    steps = {
        "A": do_a, "J": do_j, "Z": do_z, "S": do_s, "C": do_c, "D": do_d, "E": do_e, "F": do_f,
        "R": do_r, "H": do_h, "W": do_w, "FIN": do_fin,
    }
    weights_here = False
    for step in ORDER:
        if step[0] == "C" and not weights_here:
            fetch[2].wait()
            fetch[3].wait()
            weights_here = True
        steps[step[0]](*step[1:])


def hand_out(*refs):
    results, outputs, held, arrive, leave = refs[0:4], refs[4:8], refs[8:12], refs[12], refs[13]
    order = (2, 3, 0, 1)
    fetches = {i: pltpu.make_async_copy(results[i], held[i], arrive.at[i]) for i in order}
    stores = {i: pltpu.make_async_copy(held[i], outputs[i], leave.at[i]) for i in order}
    for i in order:
        fetches[i].start()
    for i in order:
        fetches[i].wait()
        stores[i].start()
    for i in order:
        stores[i].wait()


def shards(tokens, weight_in, weight_out, grad_out):
    any_space = pl.BlockSpec(memory_space=pl.ANY)
    dma = pltpu.SemaphoreType.DMA
    shapes = (
        jax.ShapeDtypeStruct((16, 1152), BF16),
        jax.ShapeDtypeStruct((16, 1152), BF16),
        jax.ShapeDtypeStruct((1152, 384), BF16),
        jax.ShapeDtypeStruct((384, 1152), BF16),
    )
    results = pl.pallas_call(
        kernel,
        out_shape=shapes,
        in_specs=[any_space] * 4,
        out_specs=(any_space,) * 4,
        scratch_shapes=[
            pltpu.VMEM((2, 8, 16, 1152), BF16),
            pltpu.VMEM((4, 2, 256, 1152), BF16),
            pltpu.VMEM((1152, 384), BF16),
            pltpu.VMEM((384, 1152), BF16),
            pltpu.VMEM((4, 4, 2, 64, 384), BF16),
            pltpu.VMEM((3, 4, 2, 64, 384), BF16),
            pltpu.VMEM((4, 2, 64, 384), BF16),
            pltpu.VMEM((4, 2, 64, 384), BF16),
            pltpu.VMEM((4, 2, 4, 64, 384), BF16),
            pltpu.VMEM((384, 1024), BF16),
            pltpu.VMEM((384, 1024), BF16),
            pltpu.VMEM((4, 2, 128, 1152), BF16),
            pltpu.VMEM((4, 2, 128, 1152), BF16),
            pltpu.VMEM((4, 2, 128, 1152), F32),
            pltpu.VMEM((4, 4, 2, 2, 16, 1152), BF16),
            pltpu.VMEM((4, 4, 2, 2, 16, 1152), BF16),
            pltpu.VMEM((3, 2, 16, 1152), BF16),
            pltpu.VMEM((3, 2, 16, 1152), BF16),
            pltpu.VMEM((2, 16, 1152), F32),
            pltpu.VMEM((2, 16, 1152), BF16),
            pltpu.VMEM((1152, 384), BF16),
            pltpu.VMEM((384, 1152), BF16),
            dma((8,)),
            dma, dma((3,)),
            dma, dma((1,)),
            dma, dma((3,)),
            dma, dma((12,)),
            dma, dma((4,)),
            dma, dma((4,)),
            dma, dma((4,)),
            dma, dma((8,)),
            dma, dma((32,)),
            dma, dma((3,)),
        ],
        compiler_params=pltpu.CompilerParams(
            collective_id=0, has_side_effects=True, vmem_limit_bytes=56 * 1024 * 1024
        ),
        cost_estimate=pl.CostEstimate(flops=5436000000, bytes_accessed=8000000, transcendentals=1000000),
    )(tokens.reshape(8, 16, 1152), weight_in, weight_out, grad_out.reshape(8, 16, 1152))
    return pl.pallas_call(
        hand_out,
        out_shape=shapes,
        in_specs=[any_space] * 4,
        out_specs=(any_space,) * 4,
        scratch_shapes=[*(pltpu.VMEM(shape.shape, BF16) for shape in shapes), dma((4,)), dma((4,))],
    )(*results)


def solution(mesh):
    placed = (P("dp", "row"), P("row", ("dp", "col")), P(("dp", "col"), "row"), P("dp", "row"))
    return jax.shard_map(
        shards,
        mesh=mesh,
        in_specs=placed,
        out_specs=(
            P(("dp", "col"), "row"),
            P(("dp", "col"), "row"),
            P("row", ("dp", "col")),
            P(("dp", "col"), "row"),
        ),
        check_vma=False,
    )
```

```python
import jax
import jax.numpy as jnp
from jax import lax
from jax.experimental import pallas as pl
from jax.experimental.pallas import tpu as pltpu
from jax.sharding import PartitionSpec as P

MESH = pl.DeviceIdType.MESH
BF16 = jnp.bfloat16
F32 = jnp.float32

PLACE = {0: 0, 4: 1, 7: 2, 3: 3, 1: 4, 5: 5, 2: 6, 6: 7}
ORDER = (
    ("A",), ("J",), ("Z", 1, 0, "L"), ("Z", 1, 0, "R"), ("C", 0), ("Z", 2, 0, "L"), ("Z", 2, 0, "R"),
    ("Z", 1, 1, "L"), ("Z", 1, 1, "R"), ("S", 1, 0), ("Z", 2, 1, "L"), ("Z", 2, 1, "R"), ("Z", 3, 0, "L"),
    ("Z", 3, 0, "R"), ("S", 1, 1), ("S", 2, 0), ("D", 0), ("C", 1), ("S", 2, 1), ("Z", 3, 1, "L"), ("S", 3, 0),
    ("Z", 3, 1, "R"), ("C", 2), ("D", 1), ("E", 0), ("S", 3, 1), ("C", 3), ("D", 2), ("E", 1), ("F", 0), ("D", 3),
    ("E", 2), ("R", 0, 0, "R"), ("R", 0, 0, "L"), ("F", 1), ("R", 0, 1, "R"), ("R", 0, 1, "L"), ("E", 3), ("F", 2),
    ("R", 1, 0, "R"), ("R", 1, 0, "L"), ("R", 0, 2, "R"), ("R", 0, 2, "L"), ("R", 2, 0, "R"), ("R", 1, 1, "R"),
    ("R", 2, 0, "L"), ("F", 3), ("R", 1, 1, "L"), ("R", 2, 1, "R"), ("R", 2, 1, "L"), ("R", 3, 0, "R"),
    ("R", 3, 0, "L"), ("R", 1, 2, "R"), ("R", 1, 2, "L"), ("R", 2, 2, "R"), ("R", 2, 2, "L"), ("R", 3, 1, "R"),
    ("R", 3, 1, "L"), ("W", 0), ("W", 3), ("R", 2, 3, "R"), ("R", 2, 3, "L"), ("R", 1, 3, "R"), ("R", 1, 3, "L"),
    ("H", 3), ("R", 0, 3, "R"), ("H", 2), ("W", 1), ("H", 1), ("R", 0, 3, "L"), ("W", 2), ("W", 4), ("H", 0),
    ("FIN",),
)


TWO_STEP = (3,)


def gelu_both(pre_value, grad_value):
    square = pre_value * pre_value
    tanh_part = jnp.tanh(0.7978845608 * (pre_value + 0.044715 * square * pre_value))
    inner_slope = 0.7978845608 * (1.0 + 0.134145 * square)
    value = 0.5 * pre_value * (1.0 + tanh_part)
    slope = 0.5 * (1.0 + tanh_part) + 0.5 * pre_value * (1.0 - tanh_part * tanh_part) * inner_slope
    return value, grad_value * slope


def rows_of(place, count=1):
    return pl.ds(place * 16, count * 16)


def times(left, right):
    return jnp.dot(left, right, preferred_element_type=F32)


def times_transposed(left, right):
    return lax.dot_general(left, right, (((1,), (1,)), ((), ())), preferred_element_type=F32)


def kernel(
    tokens, weight_in, weight_out, grad_out,
    layer_out, grad_tokens, grad_weight_in, grad_weight_out,
    TK, X, WI, WO, PS, PR, YS, YR, HC, HT, GT, SS, SR, OP, ZS, ZR, FS, FR, GS, GR, FO, OB, GI, GO,
    local_sem, a_send, a_recv, j_send, j_recv, c_send, c_recv, z_send, z_recv,
    p_send, p_recv, y_send, y_recv, h_send, h_recv, s_send, s_recv, r_send, r_recv, q_send, f_send, f_recv, g_send, g_recv,
):
    dp = lax.axis_index("dp")
    row = lax.axis_index("row")
    z = lax.axis_index("col")
    y, core = dp // 2, dp % 2
    half, x = row // 4, row % 4

    def device(y=y, core=core, half=half, x=x, z=z):
        return {"dp": y * 2 + core, "row": half * 4 + x, "col": z}

    sibling = device(core=1 - core)
    ring = {"R": device(z=(z + 1) % 8), "L": device(z=(z + 7) % 8)}
    across = device(half=1 - half)
    y_peer = {1: device(y=y + 1 - 2 * (y % 2)), 2: device(y=(y + 2) % 4), 3: device(y=3 - y)}
    far = device(z=(z + 4) % 8)
    far_peer = {j: {**y_peer[j], "col": (z + 4) % 8} for j in (1, 2, 3)}
    x_at = {m: (x + m) % 4 for m in (1, 2, 3)}
    x_peer = {m: device(x=x_at[m]) for m in (1, 2, 3)}

    waited = set()

    def send(src, dst, sems, index, to):
        copy = pltpu.make_async_remote_copy(
            src_ref=src, dst_ref=dst, send_sem=sems[0], recv_sem=sems[1].at[index],
            device_id=to, device_id_type=MESH,
        )
        copy.start()

    def arrived(dst, sems, index):
        if (id(sems), index) in waited:
            return
        waited.add((id(sems), index))
        pltpu.make_async_remote_copy(
            src_ref=dst, dst_ref=dst, send_sem=sems[0], recv_sem=sems[1].at[index],
            device_id=sibling, device_id_type=MESH,
        ).wait_recv()

    def all_left(ref, sems):
        pltpu.make_async_remote_copy(
            src_ref=ref, dst_ref=ref, send_sem=sems[0], recv_sem=sems[1].at[0],
            device_id=sibling, device_id_type=MESH,
        ).wait_send()

    a_sem, j_sem, c_sem, z_sem = (a_send, a_recv), (j_send, j_recv), (c_send, c_recv), (z_send, z_recv)
    p_sem, y_sem, h_sem, s_sem = (p_send, p_recv), (y_send, y_recv), (h_send, h_recv), (s_send, s_recv)
    f_sem, g_sem = (f_send, f_recv), (g_send, g_recv)
    ring_sem, two_sem = (r_send, r_recv), (q_send, r_recv)
    r_sems = [two_sem if j in TWO_STEP else ring_sem for j in range(4)]

    barrier = pltpu.get_barrier_semaphore()
    peers = [sibling, *ring.values(), *y_peer.values(), *x_peer.values()]
    peers += [across]
    peers += [far if j == 0 else far_peer[j] for j in TWO_STEP]
    for peer in peers:
        pl.semaphore_signal(barrier, inc=1, device_id=peer, device_id_type=MESH)
    fetch = [
        pltpu.make_async_copy(tokens, TK.at[0], local_sem.at[0]),
        pltpu.make_async_copy(grad_out, TK.at[1], local_sem.at[1]),
        pltpu.make_async_copy(weight_in, WI, local_sem.at[2]),
        pltpu.make_async_copy(weight_out, WO, local_sem.at[3]),
    ]
    for copy in fetch:
        copy.start()

    pl.semaphore_wait(barrier, len(peers))
    fetch[0].wait()
    fetch[1].wait()

    def fill(distances):
        for r in distances:
            for a in range(2):
                X[0, a, rows_of(PLACE[r])] = TK[a, (z + r) % 8]

    def do_a():
        fill((0, 4))
        for j in (1, 2, 3):
            send(X.at[0, :, rows_of(0, 2)], X.at[j, :, rows_of(0, 2)], a_sem, j - 1, y_peer[j])

    def do_j():
        fill((1, 2, 3, 5, 6, 7))
        send(X.at[0, :, 0:128], X.at[0, :, 128:256], j_sem, 0, sibling)

    def z_rows(s, d):
        return rows_of(2 if d == "R" else 4, 2) if s == 0 else rows_of(7 if d == "R" else 6)

    def z_arrived(j, s, d):
        arrived(X.at[j, :, z_rows(s, d)], z_sem, ((j - 1) * 2 + s) * 2 + "RL".index(d))

    def do_z(j, s, d):
        if s == 0:
            arrived(X.at[j, :, rows_of(0, 2)], a_sem, j - 1)
            source = rows_of(0, 2)
        else:
            z_arrived(j, 0, d)
            source = rows_of(2 if d == "R" else 4)
        index = ((j - 1) * 2 + s) * 2 + "RL".index(d)
        send(X.at[j, :, source], X.at[j, :, z_rows(s, d)], z_sem, index, ring[d])

    def do_s(j, part):
        if part == 0:
            arrived(X.at[j, :, rows_of(0, 2)], a_sem, j - 1)
        for d in "RL":
            z_arrived(j, part, d)
        q, n = ((0, 6), (6, 2))[part]
        send(X.at[j, :, rows_of(q, n)], X.at[j, :, rows_of(8 + q, n)], c_sem, j - 1, sibling)

    def do_c(j):
        if j == 0:
            arrived(X.at[0, :, 128:256], j_sem, 0)
        else:
            arrived(X.at[j, :, 128:256], c_sem, j - 1)
        PS[:, j, 0] = times(X[j, 0], WI[...]).astype(BF16).reshape(4, 64, 384)
        PS[:, j, 1] = times_transposed(X[j, 1], WO[...]).astype(BF16).reshape(4, 64, 384)
        for m in (2, 1, 3):
            send(PS.at[x_at[m], j], PR.at[m - 1, j], p_sem, j, x_peer[m])

    def do_d(j):
        arrived(PR.at[:, j], p_sem, j)
        total = PS[x, j].astype(F32)
        for m in (1, 2, 3):
            total = total + PR[m - 1, j].astype(F32)
        YS[j] = total.astype(BF16)
        send(YS.at[j], YR.at[j], y_sem, j, across)

    def do_e(j):
        arrived(YR.at[j], y_sem, j)
        pre, grad = (YS[j, a].astype(F32) + YR[j, a].astype(F32) for a in (0, 1))
        value, slope = gelu_both(pre, grad)
        HC[j, 0, x] = value.astype(BF16)
        HC[j, 1, x] = slope.astype(BF16)
        for m in (2, 1, 3):
            send(HC.at[j, :, x], HC.at[j, :, x], h_sem, j, x_peer[m])

    def do_f(j):
        arrived(PR.at[:, j], h_sem, j)
        for a in (0, 1):
            lhs = HC[j, a].reshape(256, 384)
            val = times(lhs, WO[...]) if a == 0 else times_transposed(lhs, WI[...])
            OP[j, a] = val[0:128]
            SS[j, a] = val[128:256].astype(BF16)
            send(SS.at[j, a], SR.at[j, a], s_sem, j * 2 + a, sibling)
        HT[:, j * 256:(j + 1) * 256] = HC[j, 0].reshape(256, 384).T
        GT[:, j * 256:(j + 1) * 256] = HC[j, 1].reshape(256, 384).T

    def r_index(j, i, d):
        return (j * 4 + i) * 2 + "RL".index(d)

    def both_cores(j, r, a):
        rows = rows_of(PLACE[r])
        return OP[j, a, rows] + SR[j, a, rows].astype(F32)

    def r_parts(j, i, d):
        direction = "RL".index(d)
        if j in TWO_STEP:
            if i == 0:
                return ((2 if d == "R" else 6, (0, 1), 0),)
            return ((1, (0, 1), 1), (5, (0, 1), 2)) if d == "R" else ((7, (0, 1), 1), (3, (0, 1), 2))
        return ((4 - i if d == "R" else 4 + i, (0, 1) if i else (direction,), i),)

    def r_ref(buffer, j, i, d):
        direction = "RL".index(d)
        if j in TWO_STEP:
            return buffer.at[j, 0, direction] if i == 0 else buffer.at[j, 1:3, direction]
        return buffer.at[j, i, direction] if i else buffer.at[j, i, direction, direction]

    def received(j, slot, d, a):
        return ZR[j, slot, "RL".index(d), a].astype(F32)

    def do_r(j, i, d):
        direction = "RL".index(d)
        for a in (0, 1) if i or j in TWO_STEP else (direction,):
            arrived(SR.at[j, a], s_sem, j * 2 + a)
        if i:
            arrived(r_ref(ZR, j, i - 1, d), r_sems[j], r_index(j, i - 1, d))
        for r, arrays, slot in r_parts(j, i, d):
            for a in arrays:
                total = both_cores(j, r, a)
                if j in TWO_STEP:
                    adds = i == 1 and slot == 1
                else:
                    adds = i > 1 or (i == 1 and a == direction)
                if adds:
                    total = total + received(j, i - 1, d, a)
                ZS[j, slot, direction, a] = total.astype(BF16)
        send(r_ref(ZS, j, i, d), r_ref(ZR, j, i, d), r_sems[j], r_index(j, i, d), ring[d])

    def do_h(j):
        last = 1 if j in TWO_STEP else 3
        for a in (0, 1):
            arrived(SR.at[j, a], s_sem, j * 2 + a)
        for d in "RL":
            arrived(r_ref(ZR, j, last, d), r_sems[j], r_index(j, last, d))
        if j in TWO_STEP:
            for a in (0, 1):
                total = both_cores(j, 4, a) + received(j, 2, "R", a) + received(j, 2, "L", a)
                GS[j, a] = total.astype(BF16)
            send(GS.at[j], GR.at[j], g_sem, j, far_peer[j] if j else far)
        for a in (0, 1):
            total = both_cores(j, 0, a) + received(j, last, "R", a) + received(j, last, "L", a)
            if j == 0:
                FO[a] = total
            else:
                FS[j - 1, a] = total.astype(BF16)
        if j:
            send(FS.at[j - 1], FR.at[j - 1], f_sem, j - 1, y_peer[j])

    def do_w(k):
        cols = pl.ds(k * 256, min(256, 1152 - k * 256))
        GI[cols, :] = times(GT[...], X[:, 0, :, cols].reshape(1024, cols.size)).T.astype(BF16)
        GO[:, cols] = times(HT[...], X[:, 1, :, cols].reshape(1024, cols.size)).astype(BF16)

    def do_fin():
        stores = [
            pltpu.make_async_copy(GI, grad_weight_in, local_sem.at[4]),
            pltpu.make_async_copy(GO, grad_weight_out, local_sem.at[5]),
        ]
        for copy in stores:
            copy.start()
        total = FO[...]
        for j in (1, 2, 3):
            arrived(FR.at[j - 1], f_sem, j - 1)
            total = total + FR[j - 1].astype(F32)
        for j in TWO_STEP:
            arrived(GR.at[j], g_sem, j)
            total = total + GR[j].astype(F32)
        OB[...] = total.astype(BF16)
        stores.append(pltpu.make_async_copy(OB.at[0], layer_out, local_sem.at[6]))
        stores.append(pltpu.make_async_copy(OB.at[1], grad_tokens, local_sem.at[7]))
        stores[2].start()
        stores[3].start()
        all_left(X.at[1:4, :, 0:32], a_sem)
        all_left(X.at[0, :, 0:128], j_sem)
        all_left(X.at[1:4, :, 0:128], c_sem)
        all_left(X.at[1:4, :, 0:96], z_sem)
        all_left(PR, p_sem)
        all_left(YS, y_sem)
        all_left(PR, h_sem)
        all_left(SS, s_sem)
        ring_batches = [j for j in range(4) if j not in TWO_STEP]
        all_left(X.at[0:len(ring_batches), :, 0:112], ring_sem)
        all_left(X.at[0:len(TWO_STEP), :, 0:96], two_sem)
        all_left(GS.at[0:len(TWO_STEP)], g_sem)
        all_left(FS, f_sem)
        for copy in stores:
            copy.wait()

    steps = {
        "A": do_a, "J": do_j, "Z": do_z, "S": do_s, "C": do_c, "D": do_d, "E": do_e, "F": do_f,
        "R": do_r, "H": do_h, "W": do_w, "FIN": do_fin,
    }
    weights_here = False
    for step in ORDER:
        if step[0] == "C" and not weights_here:
            fetch[2].wait()
            fetch[3].wait()
            weights_here = True
        steps[step[0]](*step[1:])


def hand_out(*refs):
    results, outputs, held, arrive, leave = refs[0:4], refs[4:8], refs[8:12], refs[12], refs[13]
    order = (2, 3, 0, 1)
    fetches = {i: pltpu.make_async_copy(results[i], held[i], arrive.at[i]) for i in order}
    stores = {i: pltpu.make_async_copy(held[i], outputs[i], leave.at[i]) for i in order}
    for i in order:
        fetches[i].start()
    for i in order:
        fetches[i].wait()
        stores[i].start()
    for i in order:
        stores[i].wait()


def shards(tokens, weight_in, weight_out, grad_out):
    any_space = pl.BlockSpec(memory_space=pl.ANY)
    dma = pltpu.SemaphoreType.DMA
    shapes = (
        jax.ShapeDtypeStruct((16, 1152), BF16),
        jax.ShapeDtypeStruct((16, 1152), BF16),
        jax.ShapeDtypeStruct((1152, 384), BF16),
        jax.ShapeDtypeStruct((384, 1152), BF16),
    )
    results = pl.pallas_call(
        kernel,
        out_shape=shapes,
        in_specs=[any_space] * 4,
        out_specs=(any_space,) * 4,
        scratch_shapes=[
            pltpu.VMEM((2, 8, 16, 1152), BF16),
            pltpu.VMEM((4, 2, 256, 1152), BF16),
            pltpu.VMEM((1152, 384), BF16),
            pltpu.VMEM((384, 1152), BF16),
            pltpu.VMEM((4, 4, 2, 64, 384), BF16),
            pltpu.VMEM((3, 4, 2, 64, 384), BF16),
            pltpu.VMEM((4, 2, 64, 384), BF16),
            pltpu.VMEM((4, 2, 64, 384), BF16),
            pltpu.VMEM((4, 2, 4, 64, 384), BF16),
            pltpu.VMEM((384, 1024), BF16),
            pltpu.VMEM((384, 1024), BF16),
            pltpu.VMEM((4, 2, 128, 1152), BF16),
            pltpu.VMEM((4, 2, 128, 1152), BF16),
            pltpu.VMEM((4, 2, 128, 1152), F32),
            pltpu.VMEM((4, 4, 2, 2, 16, 1152), BF16),
            pltpu.VMEM((4, 4, 2, 2, 16, 1152), BF16),
            pltpu.VMEM((3, 2, 16, 1152), BF16),
            pltpu.VMEM((3, 2, 16, 1152), BF16),
            pltpu.VMEM((4, 2, 16, 1152), BF16),
            pltpu.VMEM((4, 2, 16, 1152), BF16),
            pltpu.VMEM((2, 16, 1152), F32),
            pltpu.VMEM((2, 16, 1152), BF16),
            pltpu.VMEM((1152, 384), BF16),
            pltpu.VMEM((384, 1152), BF16),
            dma((8,)),
            dma, dma((3,)),
            dma, dma((1,)),
            dma, dma((3,)),
            dma, dma((12,)),
            dma, dma((4,)),
            dma, dma((4,)),
            dma, dma((4,)),
            dma, dma((8,)),
            dma, dma((32,)), dma,
            dma, dma((3,)),
            dma, dma((4,)),
        ],
        compiler_params=pltpu.CompilerParams(
            collective_id=0, has_side_effects=True, vmem_limit_bytes=56 * 1024 * 1024
        ),
        cost_estimate=pl.CostEstimate(flops=5436000000, bytes_accessed=8000000, transcendentals=1000000),
    )(tokens.reshape(8, 16, 1152), weight_in, weight_out, grad_out.reshape(8, 16, 1152))
    return pl.pallas_call(
        hand_out,
        out_shape=shapes,
        in_specs=[any_space] * 4,
        out_specs=(any_space,) * 4,
        scratch_shapes=[*(pltpu.VMEM(shape.shape, BF16) for shape in shapes), dma((4,)), dma((4,))],
    )(*results)


def solution(mesh):
    placed = (P("dp", "row"), P("row", ("dp", "col")), P(("dp", "col"), "row"), P("dp", "row"))
    return jax.shard_map(
        shards,
        mesh=mesh,
        in_specs=placed,
        out_specs=(
            P(("dp", "col"), "row"),
            P(("dp", "col"), "row"),
            P("row", ("dp", "col")),
            P(("dp", "col"), "row"),
        ),
        check_vma=False,
    )
```

```python
import jax
import jax.numpy as jnp
from jax import lax
from jax.experimental import pallas as pl
from jax.experimental.pallas import tpu as pltpu
from jax.sharding import PartitionSpec as P

MESH = pl.DeviceIdType.MESH
BF16 = jnp.bfloat16
F32 = jnp.float32

PLACE = {0: 0, 4: 1, 7: 2, 3: 3, 1: 4, 5: 5, 2: 6, 6: 7}
ORDER = (
    ("A",), ("J",), ("Z", 1, 0, "R"), ("Z", 1, 0, "L"), ("C", 0, 0), ("Z", 2, 0, "R"), ("Z", 2, 0, "L"),
    ("C", 0, 1), ("Z", 1, 1, "R"), ("Z", 1, 1, "L"), ("S", 1, 0), ("Z", 2, 1, "R"), ("Z", 2, 1, "L"),
    ("Z", 3, 0, "R"), ("Z", 3, 0, "L"), ("S", 1, 1), ("D", 0), ("S", 2, 0), ("S", 2, 1), ("C", 1, 0), ("C", 1, 1),
    ("Z", 3, 1, "R"), ("Z", 3, 1, "L"), ("S", 3, 0), ("C", 2, 0), ("C", 2, 1), ("S", 3, 1), ("D", 1), ("C", 3, 0),
    ("C", 3, 1), ("D", 2), ("E", 1), ("D", 3), ("E", 2), ("F", 1, 0), ("F", 1, 1), ("E", 3), ("E", 0), ("F", 2, 0),
    ("F", 2, 1), ("K",), ("T", 1), ("T", 2), ("R", 2, 0, "R"), ("F", 3, 0), ("R", 2, 0, "L"), ("F", 3, 1),
    ("T", 3), ("R", 2, 1, "R"), ("R", 2, 1, "L"), ("R", 3, 0, "R"), ("F", 0, 0), ("R", 3, 0, "L"), ("F", 0, 1),
    ("R", 2, 2, "R"), ("R", 2, 2, "L"), ("R", 3, 1, "R"), ("T", 0), ("R", 3, 1, "L"), ("R", 0, 0, "R"),
    ("W", 0, 1), ("R", 0, 0, "L"), ("R", 2, 3, "R"), ("R", 2, 3, "L"), ("W", 4, 1), ("R", 3, 2, "R"),
    ("R", 3, 2, "L"), ("R", 0, 1, "R"), ("R", 0, 1, "L"), ("W", 1, 1), ("W", 2, 0), ("H", 2), ("R", 3, 3, "R"),
    ("R", 3, 3, "L"), ("R", 0, 2, "R"), ("R", 0, 2, "L"), ("W", 3, 0), ("W", 1, 0), ("H", 3), ("W", 4, 0),
    ("R", 0, 3, "R"), ("R", 0, 3, "L"), ("W", 3, 1), ("W", 2, 1), ("W", 0, 0), ("H", 0), ("FIN",),
)


TWO_STEP = ()
RETURNED = (2, 3)
FOLD_INTO = 0


def gelu_both(pre_value, grad_value):
    square = pre_value * pre_value
    tanh_part = jnp.tanh(0.7978845608 * (pre_value + 0.044715 * square * pre_value))
    inner_slope = 0.7978845608 * (1.0 + 0.134145 * square)
    value = 0.5 * pre_value * (1.0 + tanh_part)
    slope = 0.5 * (1.0 + tanh_part) + 0.5 * pre_value * (1.0 - tanh_part * tanh_part) * inner_slope
    return value, grad_value * slope


def rows_of(place, count=1):
    return pl.ds(place * 16, count * 16)


def times(left, right):
    return jnp.dot(left, right, preferred_element_type=F32)


def times_transposed(left, right):
    return lax.dot_general(left, right, (((1,), (1,)), ((), ())), preferred_element_type=F32)


def kernel(
    tokens, weight_in, weight_out, grad_out,
    layer_out, grad_tokens, grad_weight_in, grad_weight_out,
    TK, X, WI, WO, PS, PR, YS, YR, HC, HT, GT, SS, SR, OP, ZS, ZR, FS, FR, GS, GR, KS, KR, FO, OB, GI, GO,
    local_sem, a_send, a_recv, j_send, j_recv, c_send, c_recv, z_send, z_recv,
    p_send, p_recv, y_send, y_recv, h_send, h_recv, s_send, s_recv, r_send, r_recv, q_send, f_send, f_recv, g_send, g_recv, k_send, k_recv,
):
    dp = lax.axis_index("dp")
    row = lax.axis_index("row")
    z = lax.axis_index("col")
    y, core = dp // 2, dp % 2
    half, x = row // 4, row % 4

    def device(y=y, core=core, half=half, x=x, z=z):
        return {"dp": y * 2 + core, "row": half * 4 + x, "col": z}

    sibling = device(core=1 - core)
    ring = {"R": device(z=(z + 1) % 8), "L": device(z=(z + 7) % 8)}
    across = device(half=1 - half)
    y_peer = {1: device(y=y + 1 - 2 * (y % 2)), 2: device(y=(y + 2) % 4), 3: device(y=3 - y)}
    far = device(z=(z + 4) % 8)
    far_peer = {j: {**y_peer[j], "col": (z + 4) % 8} for j in (1, 2, 3)}
    x_at = {m: (x + m) % 4 for m in (1, 2, 3)}
    x_peer = {m: device(x=x_at[m]) for m in (1, 2, 3)}

    waited = set()

    def send(src, dst, sems, index, to):
        copy = pltpu.make_async_remote_copy(
            src_ref=src, dst_ref=dst, send_sem=sems[0], recv_sem=sems[1].at[index],
            device_id=to, device_id_type=MESH,
        )
        copy.start()

    def arrived(dst, sems, index):
        if (id(sems), index) in waited:
            return
        waited.add((id(sems), index))
        pltpu.make_async_remote_copy(
            src_ref=dst, dst_ref=dst, send_sem=sems[0], recv_sem=sems[1].at[index],
            device_id=sibling, device_id_type=MESH,
        ).wait_recv()

    def all_left(ref, sems):
        pltpu.make_async_remote_copy(
            src_ref=ref, dst_ref=ref, send_sem=sems[0], recv_sem=sems[1].at[0],
            device_id=sibling, device_id_type=MESH,
        ).wait_send()

    a_sem, j_sem, c_sem, z_sem = (a_send, a_recv), (j_send, j_recv), (c_send, c_recv), (z_send, z_recv)
    p_sem, y_sem, h_sem, s_sem = (p_send, p_recv), (y_send, y_recv), (h_send, h_recv), (s_send, s_recv)
    f_sem, g_sem, k_sem = (f_send, f_recv), (g_send, g_recv), (k_send, k_recv)
    ring_sem, two_sem = (r_send, r_recv), (q_send, r_recv)
    r_sems = [two_sem if j in TWO_STEP else ring_sem for j in range(4)]

    barrier = pltpu.get_barrier_semaphore()
    peers = [sibling, *ring.values(), *y_peer.values(), *x_peer.values()]
    peers += [across]
    peers += [far if j == 0 else far_peer[j] for j in TWO_STEP]
    for peer in peers:
        pl.semaphore_signal(barrier, inc=1, device_id=peer, device_id_type=MESH)
    fetch = [
        pltpu.make_async_copy(tokens, TK.at[0], local_sem.at[0]),
        pltpu.make_async_copy(grad_out, TK.at[1], local_sem.at[1]),
        pltpu.make_async_copy(weight_in, WI, local_sem.at[2]),
        pltpu.make_async_copy(weight_out, WO, local_sem.at[3]),
    ]
    for copy in fetch:
        copy.start()

    pl.semaphore_wait(barrier, len(peers))
    fetch[0].wait()
    fetch[1].wait()

    def fill(distances):
        for r in distances:
            for a in range(2):
                X[0, a, rows_of(PLACE[r])] = TK[a, (z + r) % 8]

    def do_a():
        fill((0, 4))
        for j in (1, 2, 3):
            send(X.at[0, :, rows_of(0, 2)], X.at[j, :, rows_of(0, 2)], a_sem, j - 1, y_peer[j])

    def do_j():
        fill((1, 2, 3, 5, 6, 7))
        send(X.at[0, :, 0:128], X.at[0, :, 128:256], j_sem, 0, sibling)

    def z_rows(s, d):
        return rows_of(2 if d == "R" else 4, 2) if s == 0 else rows_of(7 if d == "R" else 6)

    def z_arrived(j, s, d):
        arrived(X.at[j, :, z_rows(s, d)], z_sem, ((j - 1) * 2 + s) * 2 + "RL".index(d))

    def do_z(j, s, d):
        if s == 0:
            arrived(X.at[j, :, rows_of(0, 2)], a_sem, j - 1)
            source = rows_of(0, 2)
        else:
            z_arrived(j, 0, d)
            source = rows_of(2 if d == "R" else 4)
        index = ((j - 1) * 2 + s) * 2 + "RL".index(d)
        send(X.at[j, :, source], X.at[j, :, z_rows(s, d)], z_sem, index, ring[d])

    def do_s(j, part):
        if part == 0:
            arrived(X.at[j, :, rows_of(0, 2)], a_sem, j - 1)
        for d in "RL":
            z_arrived(j, part, d)
        q, n = ((0, 6), (6, 2))[part]
        send(X.at[j, :, rows_of(q, n)], X.at[j, :, rows_of(8 + q, n)], c_sem, j - 1, sibling)

    def do_c(j, a):
        if j == 0:
            arrived(X.at[0, :, 128:256], j_sem, 0)
        else:
            arrived(X.at[j, :, 128:256], c_sem, j - 1)
        val = times(X[j, 0], WI[...]) if a == 0 else times_transposed(X[j, 1], WO[...])
        PS[:, j, a] = val.astype(BF16).reshape(4, 64, 384)
        if a == 1:
            for m in (2, 1, 3):
                send(PS.at[x_at[m], j], PR.at[m - 1, j], p_sem, j, x_peer[m])

    def do_d(j):
        arrived(PR.at[:, j], p_sem, j)
        total = PS[x, j].astype(F32)
        for m in (1, 2, 3):
            total = total + PR[m - 1, j].astype(F32)
        YS[j] = total.astype(BF16)
        send(YS.at[j], YR.at[j], y_sem, j, across)

    def do_e(j):
        arrived(YR.at[j], y_sem, j)
        pre, grad = (YS[j, a].astype(F32) + YR[j, a].astype(F32) for a in (0, 1))
        value, slope = gelu_both(pre, grad)
        HC[j, 0, x] = value.astype(BF16)
        HC[j, 1, x] = slope.astype(BF16)
        for m in (2, 1, 3):
            send(HC.at[j, :, x], HC.at[j, :, x], h_sem, j, x_peer[m])

    def do_f(j, a):
        arrived(PR.at[:, j], h_sem, j)
        lhs = HC[j, a].reshape(256, 384)
        val = times(lhs, WO[...]) if a == 0 else times_transposed(lhs, WI[...])
        OP[j, a] = val[0:128]
        SS[j, a] = val[128:256].astype(BF16)
        send(SS.at[j, a], SR.at[j, a], s_sem, j * 2 + a, sibling)

    def do_t(j):
        HT[:, j * 256:(j + 1) * 256] = HC[j, 0].reshape(256, 384).T
        GT[:, j * 256:(j + 1) * 256] = HC[j, 1].reshape(256, 384).T

    def r_index(j, i, d):
        return (j * 4 + i) * 2 + "RL".index(d)

    def here(j, arrays):
        for a in arrays:
            arrived(SR.at[j, a], s_sem, j * 2 + a)
            if j == FOLD_INTO:
                arrived(KR.at[a], k_sem, a)

    def both_cores(j, r, a):
        rows = rows_of(PLACE[r])
        total = OP[j, a, rows] + SR[j, a, rows].astype(F32)
        if j == FOLD_INTO:
            total = total + KR[a, rows].astype(F32)
        return total

    def do_k():
        here(1, (0, 1))
        for a in (0, 1):
            KS[a] = (OP[1, a] + SR[1, a].astype(F32)).astype(BF16)
            send(KS.at[a], KR.at[a], k_sem, a, y_peer[1])

    def r_parts(j, i, d):
        direction = "RL".index(d)
        if j in TWO_STEP:
            if i == 0:
                return ((2 if d == "R" else 6, (0, 1), 0),)
            return ((1, (0, 1), 1), (5, (0, 1), 2)) if d == "R" else ((7, (0, 1), 1), (3, (0, 1), 2))
        return ((4 - i if d == "R" else 4 + i, (0, 1) if i else (direction,), i),)

    def r_ref(buffer, j, i, d):
        direction = "RL".index(d)
        if j in TWO_STEP:
            return buffer.at[j, 0, direction] if i == 0 else buffer.at[j, 1:3, direction]
        return buffer.at[j, i, direction] if i else buffer.at[j, i, direction, direction]

    def received(j, slot, d, a):
        return ZR[j, slot, "RL".index(d), a].astype(F32)

    def do_r(j, i, d):
        direction = "RL".index(d)
        here(j, (0, 1) if i or j in TWO_STEP else (direction,))
        if i:
            arrived(r_ref(ZR, j, i - 1, d), r_sems[j], r_index(j, i - 1, d))
        for r, arrays, slot in r_parts(j, i, d):
            for a in arrays:
                total = both_cores(j, r, a)
                if j in TWO_STEP:
                    adds = i == 1 and slot == 1
                else:
                    adds = i > 1 or (i == 1 and a == direction)
                if adds:
                    total = total + received(j, i - 1, d, a)
                ZS[j, slot, direction, a] = total.astype(BF16)
        send(r_ref(ZS, j, i, d), r_ref(ZR, j, i, d), r_sems[j], r_index(j, i, d), ring[d])

    def do_h(j):
        last = 1 if j in TWO_STEP else 3
        here(j, (0, 1))
        for d in "RL":
            arrived(r_ref(ZR, j, last, d), r_sems[j], r_index(j, last, d))
        if j in TWO_STEP:
            for a in (0, 1):
                total = both_cores(j, 4, a) + received(j, 2, "R", a) + received(j, 2, "L", a)
                GS[j, a] = total.astype(BF16)
            send(GS.at[j], GR.at[j], g_sem, j, far_peer[j] if j else far)
        for a in (0, 1):
            total = both_cores(j, 0, a) + received(j, last, "R", a) + received(j, last, "L", a)
            if j == 0:
                FO[a] = total
            else:
                FS[j - 1, a] = total.astype(BF16)
        if j:
            send(FS.at[j - 1], FR.at[j - 1], f_sem, j - 1, y_peer[j])

    def do_w(k, which):
        cols = pl.ds(k * 256, min(256, 1152 - k * 256))
        rhs = X[:, which, :, cols].reshape(1024, cols.size)
        if which == 0:
            GI[cols, :] = times(GT[...], rhs).T.astype(BF16)
        else:
            GO[:, cols] = times(HT[...], rhs).astype(BF16)

    def do_fin():
        stores = [
            pltpu.make_async_copy(GI, grad_weight_in, local_sem.at[4]),
            pltpu.make_async_copy(GO, grad_weight_out, local_sem.at[5]),
        ]
        for copy in stores:
            copy.start()
        total = FO[...]
        for j in RETURNED:
            arrived(FR.at[j - 1], f_sem, j - 1)
            total = total + FR[j - 1].astype(F32)
        for j in TWO_STEP:
            arrived(GR.at[j], g_sem, j)
            total = total + GR[j].astype(F32)
        OB[...] = total.astype(BF16)
        stores.append(pltpu.make_async_copy(OB.at[0], layer_out, local_sem.at[6]))
        stores.append(pltpu.make_async_copy(OB.at[1], grad_tokens, local_sem.at[7]))
        stores[2].start()
        stores[3].start()
        all_left(X.at[1:4, :, 0:32], a_sem)
        all_left(X.at[0, :, 0:128], j_sem)
        all_left(X.at[1:4, :, 0:128], c_sem)
        all_left(X.at[1:4, :, 0:96], z_sem)
        all_left(PR, p_sem)
        all_left(YS, y_sem)
        all_left(PR, h_sem)
        all_left(SS, s_sem)
        ring_batches = [j for j in (0, *RETURNED) if j not in TWO_STEP]
        all_left(X.at[0:len(ring_batches), :, 0:112], ring_sem)
        if TWO_STEP:
            all_left(X.at[0:len(TWO_STEP), :, 0:96], two_sem)
            all_left(GS.at[0:len(TWO_STEP)], g_sem)
        all_left(FS.at[0:len(RETURNED)], f_sem)
        all_left(KS, k_sem)
        for copy in stores:
            copy.wait()

    steps = {
        "A": do_a, "J": do_j, "Z": do_z, "S": do_s, "C": do_c, "D": do_d, "E": do_e, "F": do_f,
        "R": do_r, "H": do_h, "W": do_w, "T": do_t, "K": do_k, "FIN": do_fin,
    }
    weights_here = False
    for step in ORDER:
        if step[0] == "C" and not weights_here:
            fetch[2].wait()
            fetch[3].wait()
            weights_here = True
        steps[step[0]](*step[1:])


def hand_out(*refs):
    results, outputs, held, arrive, leave = refs[0:4], refs[4:8], refs[8:12], refs[12], refs[13]
    order = (2, 3, 0, 1)
    fetches = {i: pltpu.make_async_copy(results[i], held[i], arrive.at[i]) for i in order}
    stores = {i: pltpu.make_async_copy(held[i], outputs[i], leave.at[i]) for i in order}
    for i in order:
        fetches[i].start()
    for i in order:
        fetches[i].wait()
        stores[i].start()
    for i in order:
        stores[i].wait()


def shards(tokens, weight_in, weight_out, grad_out):
    any_space = pl.BlockSpec(memory_space=pl.ANY)
    dma = pltpu.SemaphoreType.DMA
    shapes = (
        jax.ShapeDtypeStruct((16, 1152), BF16),
        jax.ShapeDtypeStruct((16, 1152), BF16),
        jax.ShapeDtypeStruct((1152, 384), BF16),
        jax.ShapeDtypeStruct((384, 1152), BF16),
    )
    results = pl.pallas_call(
        kernel,
        out_shape=shapes,
        in_specs=[any_space] * 4,
        out_specs=(any_space,) * 4,
        scratch_shapes=[
            pltpu.VMEM((2, 8, 16, 1152), BF16),
            pltpu.VMEM((4, 2, 256, 1152), BF16),
            pltpu.VMEM((1152, 384), BF16),
            pltpu.VMEM((384, 1152), BF16),
            pltpu.VMEM((4, 4, 2, 64, 384), BF16),
            pltpu.VMEM((3, 4, 2, 64, 384), BF16),
            pltpu.VMEM((4, 2, 64, 384), BF16),
            pltpu.VMEM((4, 2, 64, 384), BF16),
            pltpu.VMEM((4, 2, 4, 64, 384), BF16),
            pltpu.VMEM((384, 1024), BF16),
            pltpu.VMEM((384, 1024), BF16),
            pltpu.VMEM((4, 2, 128, 1152), BF16),
            pltpu.VMEM((4, 2, 128, 1152), BF16),
            pltpu.VMEM((4, 2, 128, 1152), F32),
            pltpu.VMEM((4, 4, 2, 2, 16, 1152), BF16),
            pltpu.VMEM((4, 4, 2, 2, 16, 1152), BF16),
            pltpu.VMEM((3, 2, 16, 1152), BF16),
            pltpu.VMEM((3, 2, 16, 1152), BF16),
            pltpu.VMEM((4, 2, 16, 1152), BF16),
            pltpu.VMEM((4, 2, 16, 1152), BF16),
            pltpu.VMEM((2, 128, 1152), BF16),
            pltpu.VMEM((2, 128, 1152), BF16),
            pltpu.VMEM((2, 16, 1152), F32),
            pltpu.VMEM((2, 16, 1152), BF16),
            pltpu.VMEM((1152, 384), BF16),
            pltpu.VMEM((384, 1152), BF16),
            dma((8,)),
            dma, dma((3,)),
            dma, dma((1,)),
            dma, dma((3,)),
            dma, dma((12,)),
            dma, dma((4,)),
            dma, dma((4,)),
            dma, dma((4,)),
            dma, dma((8,)),
            dma, dma((32,)), dma,
            dma, dma((3,)),
            dma, dma((4,)),
            dma, dma((2,)),
        ],
        compiler_params=pltpu.CompilerParams(
            collective_id=0, has_side_effects=True, vmem_limit_bytes=56 * 1024 * 1024
        ),
        cost_estimate=pl.CostEstimate(flops=5436000000, bytes_accessed=8000000, transcendentals=1000000),
    )(tokens.reshape(8, 16, 1152), weight_in, weight_out, grad_out.reshape(8, 16, 1152))
    return pl.pallas_call(
        hand_out,
        out_shape=shapes,
        in_specs=[any_space] * 4,
        out_specs=(any_space,) * 4,
        scratch_shapes=[*(pltpu.VMEM(shape.shape, BF16) for shape in shapes), dma((4,)), dma((4,))],
    )(*results)


def solution(mesh):
    placed = (P("dp", "row"), P("row", ("dp", "col")), P(("dp", "col"), "row"), P("dp", "row"))
    return jax.shard_map(
        shards,
        mesh=mesh,
        in_specs=placed,
        out_specs=(
            P(("dp", "col"), "row"),
            P(("dp", "col"), "row"),
            P("row", ("dp", "col")),
            P(("dp", "col"), "row"),
        ),
        check_vma=False,
    )
```

```python
import jax
import jax.numpy as jnp
from jax import lax
from jax.experimental import pallas as pl
from jax.experimental.pallas import tpu as pltpu
from jax.sharding import PartitionSpec as P

MESH = pl.DeviceIdType.MESH
BF16 = jnp.bfloat16
F32 = jnp.float32

PLACE = {0: 0, 4: 1, 7: 2, 3: 3, 1: 4, 5: 5, 2: 6, 6: 7}
ORDER = (
    ("A",), ("J",), ("C", 0, 0), ("C", 0, 1), ("Z", 1, 0, "L"), ("Z", 1, 0, "R"), ("Z", 2, 0, "R"),
    ("Z", 2, 0, "L"), ("Z", 1, 1, "R"), ("Z", 1, 1, "L"), ("D", 0), ("S", 1, 0), ("Z", 2, 1, "R"),
    ("Z", 2, 1, "L"), ("S", 1, 1), ("Z", 3, 0, "L"), ("Z", 3, 0, "R"), ("S", 2, 0), ("C", 1, 0), ("S", 2, 1),
    ("C", 1, 1), ("Z", 3, 1, "L"), ("Z", 3, 1, "R"), ("C", 2, 0), ("C", 2, 1), ("S", 3, 0), ("D", 1), ("S", 3, 1),
    ("E", 0), ("C", 3, 0), ("C", 3, 1), ("D", 2), ("F", 0, 0), ("E", 1), ("D", 3), ("F", 0, 1), ("R", 0, 0, "R"),
    ("E", 2), ("R", 0, 0, "L"), ("F", 1, 0), ("T", 0), ("F", 1, 1), ("R", 0, 1, "R"), ("R", 0, 1, "L"), ("E", 3),
    ("R", 1, 0, "R"), ("R", 1, 0, "L"), ("F", 2, 0), ("R", 0, 2, "R"), ("R", 0, 2, "L"), ("F", 2, 1),
    ("R", 1, 1, "R"), ("R", 1, 1, "L"), ("F", 3, 0), ("F", 3, 1), ("R", 2, 0, "R"), ("R", 2, 0, "L"), ("T", 3),
    ("R", 1, 2, "R"), ("R", 1, 2, "L"), ("R", 3, 0, "L"), ("R", 3, 0, "R"), ("R", 2, 1, "R"), ("R", 2, 1, "L"),
    ("T", 1), ("R", 1, 3, "R"), ("T", 2), ("W", 2, 0), ("R", 3, 1, "L"), ("R", 3, 1, "R"), ("R", 1, 3, "L"),
    ("W", 4, 0), ("W", 3, 0), ("H", 2), ("H", 3), ("W", 4, 1), ("H", 1), ("R", 0, 3, "R"), ("R", 0, 3, "L"),
    ("W", 3, 1), ("W", 0, 0), ("W", 2, 1), ("W", 0, 1), ("W", 1, 0), ("W", 1, 1), ("H", 0), ("FIN",),
)


TWO_STEP = (2,3,)
RETURNED = (1, 2, 3)
FOLD_INTO = None


def gelu_both(pre_value, grad_value):
    square = pre_value * pre_value
    tanh_part = jnp.tanh(0.7978845608 * (pre_value + 0.044715 * square * pre_value))
    inner_slope = 0.7978845608 * (1.0 + 0.134145 * square)
    value = 0.5 * pre_value * (1.0 + tanh_part)
    slope = 0.5 * (1.0 + tanh_part) + 0.5 * pre_value * (1.0 - tanh_part * tanh_part) * inner_slope
    return value, grad_value * slope


def rows_of(place, count=1):
    return pl.ds(place * 16, count * 16)


def times(left, right):
    return jnp.dot(left, right, preferred_element_type=F32)


def times_transposed(left, right):
    return lax.dot_general(left, right, (((1,), (1,)), ((), ())), preferred_element_type=F32)


def kernel(
    tokens, weight_in, weight_out, grad_out,
    layer_out, grad_tokens, grad_weight_in, grad_weight_out,
    TK, X, WI, WO, PS, PR, YS, YR, HC, HT, GT, SS, SR, OP, ZS, ZR, FS, FR, GS, GR, KS, KR, FO, OB, GI, GO,
    local_sem, a_send, a_recv, j_send, j_recv, c_send, c_recv, z_send, z_recv,
    p_send, p_recv, y_send, y_recv, h_send, h_recv, s_send, s_recv, r_send, r_recv, q_send, f_send, f_recv, g_send, g_recv, k_send, k_recv,
):
    dp = lax.axis_index("dp")
    row = lax.axis_index("row")
    z = lax.axis_index("col")
    y, core = dp // 2, dp % 2
    half, x = row // 4, row % 4

    def device(y=y, core=core, half=half, x=x, z=z):
        return {"dp": y * 2 + core, "row": half * 4 + x, "col": z}

    sibling = device(core=1 - core)
    ring = {"R": device(z=(z + 1) % 8), "L": device(z=(z + 7) % 8)}
    across = device(half=1 - half)
    y_peer = {1: device(y=y + 1 - 2 * (y % 2)), 2: device(y=(y + 2) % 4), 3: device(y=3 - y)}
    far = device(z=(z + 4) % 8)
    far_peer = {j: {**y_peer[j], "col": (z + 4) % 8} for j in (1, 2, 3)}
    x_at = {m: (x + m) % 4 for m in (1, 2, 3)}
    x_peer = {m: device(x=x_at[m]) for m in (1, 2, 3)}

    waited = set()

    def send(src, dst, sems, index, to):
        copy = pltpu.make_async_remote_copy(
            src_ref=src, dst_ref=dst, send_sem=sems[0], recv_sem=sems[1].at[index],
            device_id=to, device_id_type=MESH,
        )
        copy.start()

    def arrived(dst, sems, index):
        if (id(sems), index) in waited:
            return
        waited.add((id(sems), index))
        pltpu.make_async_remote_copy(
            src_ref=dst, dst_ref=dst, send_sem=sems[0], recv_sem=sems[1].at[index],
            device_id=sibling, device_id_type=MESH,
        ).wait_recv()

    def all_left(ref, sems):
        pltpu.make_async_remote_copy(
            src_ref=ref, dst_ref=ref, send_sem=sems[0], recv_sem=sems[1].at[0],
            device_id=sibling, device_id_type=MESH,
        ).wait_send()

    a_sem, j_sem, c_sem, z_sem = (a_send, a_recv), (j_send, j_recv), (c_send, c_recv), (z_send, z_recv)
    p_sem, y_sem, h_sem, s_sem = (p_send, p_recv), (y_send, y_recv), (h_send, h_recv), (s_send, s_recv)
    f_sem, g_sem, k_sem = (f_send, f_recv), (g_send, g_recv), (k_send, k_recv)
    ring_sem, two_sem = (r_send, r_recv), (q_send, r_recv)
    r_sems = [two_sem if j in TWO_STEP else ring_sem for j in range(4)]

    barrier = pltpu.get_barrier_semaphore()
    peers = [sibling, *ring.values(), *y_peer.values(), *x_peer.values()]
    peers += [across]
    peers += [far if j == 0 else far_peer[j] for j in TWO_STEP]
    for peer in peers:
        pl.semaphore_signal(barrier, inc=1, device_id=peer, device_id_type=MESH)
    fetch = [
        pltpu.make_async_copy(tokens, TK.at[0], local_sem.at[0]),
        pltpu.make_async_copy(grad_out, TK.at[1], local_sem.at[1]),
        pltpu.make_async_copy(weight_in, WI, local_sem.at[2]),
        pltpu.make_async_copy(weight_out, WO, local_sem.at[3]),
    ]
    for copy in fetch:
        copy.start()

    pl.semaphore_wait(barrier, len(peers))
    fetch[0].wait()
    fetch[1].wait()

    def fill(distances):
        for r in distances:
            for a in range(2):
                X[0, a, rows_of(PLACE[r])] = TK[a, (z + r) % 8]

    def do_a():
        fill((0, 4))
        for j in (1, 2, 3):
            send(X.at[0, :, rows_of(0, 2)], X.at[j, :, rows_of(0, 2)], a_sem, j - 1, y_peer[j])

    def do_j():
        fill((1, 2, 3, 5, 6, 7))
        send(X.at[0, :, 0:128], X.at[0, :, 128:256], j_sem, 0, sibling)

    def z_rows(s, d):
        return rows_of(2 if d == "R" else 4, 2) if s == 0 else rows_of(7 if d == "R" else 6)

    def z_arrived(j, s, d):
        arrived(X.at[j, :, z_rows(s, d)], z_sem, ((j - 1) * 2 + s) * 2 + "RL".index(d))

    def do_z(j, s, d):
        if s == 0:
            arrived(X.at[j, :, rows_of(0, 2)], a_sem, j - 1)
            source = rows_of(0, 2)
        else:
            z_arrived(j, 0, d)
            source = rows_of(2 if d == "R" else 4)
        index = ((j - 1) * 2 + s) * 2 + "RL".index(d)
        send(X.at[j, :, source], X.at[j, :, z_rows(s, d)], z_sem, index, ring[d])

    def do_s(j, part):
        if part == 0:
            arrived(X.at[j, :, rows_of(0, 2)], a_sem, j - 1)
        for d in "RL":
            z_arrived(j, part, d)
        q, n = ((0, 6), (6, 2))[part]
        send(X.at[j, :, rows_of(q, n)], X.at[j, :, rows_of(8 + q, n)], c_sem, j - 1, sibling)

    def do_c(j, a):
        if j == 0:
            arrived(X.at[0, :, 128:256], j_sem, 0)
        else:
            arrived(X.at[j, :, 128:256], c_sem, j - 1)
        val = times(X[j, 0], WI[...]) if a == 0 else times_transposed(X[j, 1], WO[...])
        PS[:, j, a] = val.astype(BF16).reshape(4, 64, 384)
        if a == 1:
            for m in (2, 1, 3):
                send(PS.at[x_at[m], j], PR.at[m - 1, j], p_sem, j, x_peer[m])

    def do_d(j):
        arrived(PR.at[:, j], p_sem, j)
        total = PS[x, j].astype(F32)
        for m in (1, 2, 3):
            total = total + PR[m - 1, j].astype(F32)
        YS[j] = total.astype(BF16)
        send(YS.at[j], YR.at[j], y_sem, j, across)

    def do_e(j):
        arrived(YR.at[j], y_sem, j)
        pre, grad = (YS[j, a].astype(F32) + YR[j, a].astype(F32) for a in (0, 1))
        value, slope = gelu_both(pre, grad)
        HC[j, 0, x] = value.astype(BF16)
        HC[j, 1, x] = slope.astype(BF16)
        for m in (2, 1, 3):
            send(HC.at[j, :, x], HC.at[j, :, x], h_sem, j, x_peer[m])

    def do_f(j, a):
        arrived(PR.at[:, j], h_sem, j)
        lhs = HC[j, a].reshape(256, 384)
        val = times(lhs, WO[...]) if a == 0 else times_transposed(lhs, WI[...])
        OP[j, a] = val[0:128]
        SS[j, a] = val[128:256].astype(BF16)
        send(SS.at[j, a], SR.at[j, a], s_sem, j * 2 + a, sibling)

    def do_t(j):
        HT[:, j * 256:(j + 1) * 256] = HC[j, 0].reshape(256, 384).T
        GT[:, j * 256:(j + 1) * 256] = HC[j, 1].reshape(256, 384).T

    def r_index(j, i, d):
        return (j * 4 + i) * 2 + "RL".index(d)

    def here(j, arrays):
        for a in arrays:
            arrived(SR.at[j, a], s_sem, j * 2 + a)
            if j == FOLD_INTO:
                arrived(KR.at[a], k_sem, a)

    def both_cores(j, r, a):
        rows = rows_of(PLACE[r])
        total = OP[j, a, rows] + SR[j, a, rows].astype(F32)
        if j == FOLD_INTO:
            total = total + KR[a, rows].astype(F32)
        return total

    def do_k():
        here(1, (0, 1))
        for a in (0, 1):
            KS[a] = (OP[1, a] + SR[1, a].astype(F32)).astype(BF16)
            send(KS.at[a], KR.at[a], k_sem, a, y_peer[1])

    def r_parts(j, i, d):
        direction = "RL".index(d)
        if j in TWO_STEP:
            if i == 0:
                return ((2 if d == "R" else 6, (0, 1), 0),)
            return ((1, (0, 1), 1), (5, (0, 1), 2)) if d == "R" else ((7, (0, 1), 1), (3, (0, 1), 2))
        return ((4 - i if d == "R" else 4 + i, (0, 1) if i else (direction,), i),)

    def r_ref(buffer, j, i, d):
        direction = "RL".index(d)
        if j in TWO_STEP:
            return buffer.at[j, 0, direction] if i == 0 else buffer.at[j, 1:3, direction]
        return buffer.at[j, i, direction] if i else buffer.at[j, i, direction, direction]

    def received(j, slot, d, a):
        return ZR[j, slot, "RL".index(d), a].astype(F32)

    def do_r(j, i, d):
        direction = "RL".index(d)
        here(j, (0, 1) if i or j in TWO_STEP else (direction,))
        if i:
            arrived(r_ref(ZR, j, i - 1, d), r_sems[j], r_index(j, i - 1, d))
        for r, arrays, slot in r_parts(j, i, d):
            for a in arrays:
                total = both_cores(j, r, a)
                if j in TWO_STEP:
                    adds = i == 1 and slot == 1
                else:
                    adds = i > 1 or (i == 1 and a == direction)
                if adds:
                    total = total + received(j, i - 1, d, a)
                ZS[j, slot, direction, a] = total.astype(BF16)
        send(r_ref(ZS, j, i, d), r_ref(ZR, j, i, d), r_sems[j], r_index(j, i, d), ring[d])

    def do_h(j):
        last = 1 if j in TWO_STEP else 3
        here(j, (0, 1))
        for d in "RL":
            arrived(r_ref(ZR, j, last, d), r_sems[j], r_index(j, last, d))
        if j in TWO_STEP:
            for a in (0, 1):
                total = both_cores(j, 4, a) + received(j, 2, "R", a) + received(j, 2, "L", a)
                GS[j, a] = total.astype(BF16)
            send(GS.at[j], GR.at[j], g_sem, j, far_peer[j] if j else far)
        for a in (0, 1):
            total = both_cores(j, 0, a) + received(j, last, "R", a) + received(j, last, "L", a)
            if j == 0:
                FO[a] = total
            else:
                FS[j - 1, a] = total.astype(BF16)
        if j:
            send(FS.at[j - 1], FR.at[j - 1], f_sem, j - 1, y_peer[j])

    def do_w(k, which):
        cols = pl.ds(k * 256, min(256, 1152 - k * 256))
        rhs = X[:, which, :, cols].reshape(1024, cols.size)
        if which == 0:
            GI[cols, :] = times(GT[...], rhs).T.astype(BF16)
        else:
            GO[:, cols] = times(HT[...], rhs).astype(BF16)

    def do_fin():
        stores = [
            pltpu.make_async_copy(GI, grad_weight_in, local_sem.at[4]),
            pltpu.make_async_copy(GO, grad_weight_out, local_sem.at[5]),
        ]
        for copy in stores:
            copy.start()
        total = FO[...]
        for j in RETURNED:
            arrived(FR.at[j - 1], f_sem, j - 1)
            total = total + FR[j - 1].astype(F32)
        for j in TWO_STEP:
            arrived(GR.at[j], g_sem, j)
            total = total + GR[j].astype(F32)
        OB[...] = total.astype(BF16)
        stores.append(pltpu.make_async_copy(OB.at[0], layer_out, local_sem.at[6]))
        stores.append(pltpu.make_async_copy(OB.at[1], grad_tokens, local_sem.at[7]))
        stores[2].start()
        stores[3].start()
        all_left(X.at[1:4, :, 0:32], a_sem)
        all_left(X.at[0, :, 0:128], j_sem)
        all_left(X.at[1:4, :, 0:128], c_sem)
        all_left(X.at[1:4, :, 0:96], z_sem)
        all_left(PR, p_sem)
        all_left(YS, y_sem)
        all_left(PR, h_sem)
        all_left(SS, s_sem)
        ring_batches = [j for j in (0, *RETURNED) if j not in TWO_STEP]
        all_left(X.at[0:len(ring_batches), :, 0:112], ring_sem)
        if TWO_STEP:
            all_left(X.at[0:len(TWO_STEP), :, 0:96], two_sem)
            all_left(GS.at[0:len(TWO_STEP)], g_sem)
        all_left(FS.at[0:len(RETURNED)], f_sem)
        for copy in stores:
            copy.wait()

    steps = {
        "A": do_a, "J": do_j, "Z": do_z, "S": do_s, "C": do_c, "D": do_d, "E": do_e, "F": do_f,
        "R": do_r, "H": do_h, "W": do_w, "T": do_t, "K": do_k, "FIN": do_fin,
    }
    weights_here = False
    for step in ORDER:
        if step[0] == "C" and not weights_here:
            fetch[2].wait()
            fetch[3].wait()
            weights_here = True
        steps[step[0]](*step[1:])


def hand_out(*refs):
    results, outputs, held, arrive, leave = refs[0:4], refs[4:8], refs[8:12], refs[12], refs[13]
    order = (2, 3, 0, 1)
    fetches = {i: pltpu.make_async_copy(results[i], held[i], arrive.at[i]) for i in order}
    stores = {i: pltpu.make_async_copy(held[i], outputs[i], leave.at[i]) for i in order}
    for i in order:
        fetches[i].start()
    for i in order:
        fetches[i].wait()
        stores[i].start()
    for i in order:
        stores[i].wait()


def shards(tokens, weight_in, weight_out, grad_out):
    any_space = pl.BlockSpec(memory_space=pl.ANY)
    dma = pltpu.SemaphoreType.DMA
    shapes = (
        jax.ShapeDtypeStruct((16, 1152), BF16),
        jax.ShapeDtypeStruct((16, 1152), BF16),
        jax.ShapeDtypeStruct((1152, 384), BF16),
        jax.ShapeDtypeStruct((384, 1152), BF16),
    )
    results = pl.pallas_call(
        kernel,
        out_shape=shapes,
        in_specs=[any_space] * 4,
        out_specs=(any_space,) * 4,
        scratch_shapes=[
            pltpu.VMEM((2, 8, 16, 1152), BF16),
            pltpu.VMEM((4, 2, 256, 1152), BF16),
            pltpu.VMEM((1152, 384), BF16),
            pltpu.VMEM((384, 1152), BF16),
            pltpu.VMEM((4, 4, 2, 64, 384), BF16),
            pltpu.VMEM((3, 4, 2, 64, 384), BF16),
            pltpu.VMEM((4, 2, 64, 384), BF16),
            pltpu.VMEM((4, 2, 64, 384), BF16),
            pltpu.VMEM((4, 2, 4, 64, 384), BF16),
            pltpu.VMEM((384, 1024), BF16),
            pltpu.VMEM((384, 1024), BF16),
            pltpu.VMEM((4, 2, 128, 1152), BF16),
            pltpu.VMEM((4, 2, 128, 1152), BF16),
            pltpu.VMEM((4, 2, 128, 1152), F32),
            pltpu.VMEM((4, 4, 2, 2, 16, 1152), BF16),
            pltpu.VMEM((4, 4, 2, 2, 16, 1152), BF16),
            pltpu.VMEM((3, 2, 16, 1152), BF16),
            pltpu.VMEM((3, 2, 16, 1152), BF16),
            pltpu.VMEM((4, 2, 16, 1152), BF16),
            pltpu.VMEM((4, 2, 16, 1152), BF16),
            pltpu.VMEM((2, 128, 1152), BF16),
            pltpu.VMEM((2, 128, 1152), BF16),
            pltpu.VMEM((2, 16, 1152), F32),
            pltpu.VMEM((2, 16, 1152), BF16),
            pltpu.VMEM((1152, 384), BF16),
            pltpu.VMEM((384, 1152), BF16),
            dma((8,)),
            dma, dma((3,)),
            dma, dma((1,)),
            dma, dma((3,)),
            dma, dma((12,)),
            dma, dma((4,)),
            dma, dma((4,)),
            dma, dma((4,)),
            dma, dma((8,)),
            dma, dma((32,)), dma,
            dma, dma((3,)),
            dma, dma((4,)),
            dma, dma((2,)),
        ],
        compiler_params=pltpu.CompilerParams(
            collective_id=0, has_side_effects=True, vmem_limit_bytes=56 * 1024 * 1024
        ),
        cost_estimate=pl.CostEstimate(flops=5436000000, bytes_accessed=8000000, transcendentals=1000000),
    )(tokens.reshape(8, 16, 1152), weight_in, weight_out, grad_out.reshape(8, 16, 1152))
    return pl.pallas_call(
        hand_out,
        out_shape=shapes,
        in_specs=[any_space] * 4,
        out_specs=(any_space,) * 4,
        scratch_shapes=[*(pltpu.VMEM(shape.shape, BF16) for shape in shapes), dma((4,)), dma((4,))],
    )(*results)


def solution(mesh):
    placed = (P("dp", "row"), P("row", ("dp", "col")), P(("dp", "col"), "row"), P("dp", "row"))
    return jax.shard_map(
        shards,
        mesh=mesh,
        in_specs=placed,
        out_specs=(
            P(("dp", "col"), "row"),
            P(("dp", "col"), "row"),
            P("row", ("dp", "col")),
            P(("dp", "col"), "row"),
        ),
        check_vma=False,
    )
```

```python
import jax
import jax.numpy as jnp
from jax import lax
from jax.experimental import pallas as pl
from jax.experimental.pallas import tpu as pltpu
from jax.sharding import PartitionSpec as P

MESH = pl.DeviceIdType.MESH
BF16 = jnp.bfloat16
F32 = jnp.float32

PLACE = {0: 0, 4: 1, 7: 2, 3: 3, 1: 4, 5: 5, 2: 6, 6: 7}
ORDER = (
    ("A",), ("J",), ("Z", 1, 0, "R"), ("Z", 1, 0, "L"), ("C", 0), ("Z", 1, 1, "R"), ("Z", 1, 1, "L"), ("S", 1, 0),
    ("Z", 2, 0, "R"), ("Z", 2, 0, "L"), ("S", 1, 1), ("D", 0), ("C", 1), ("Z", 2, 1, "R"), ("Z", 2, 1, "L"),
    ("Z", 3, 0, "L"), ("Z", 3, 0, "R"), ("S", 2, 0), ("E", 0), ("S", 2, 1), ("D", 1), ("Z", 3, 1, "R"),
    ("Z", 3, 1, "L"), ("S", 3, 0), ("C", 2), ("S", 3, 1), ("F", 0), ("C", 3), ("D", 2), ("R", 0, 0, "R"),
    ("R", 0, 0, "L"), ("E", 1), ("R", 0, 1, "R"), ("D", 3), ("R", 0, 1, "L"), ("E", 2), ("R", 0, 2, "R"), ("F", 1),
    ("R", 0, 2, "L"), ("E", 3), ("F", 2), ("R", 1, 0, "R"), ("R", 1, 0, "L"), ("R", 2, 0, "R"), ("R", 1, 1, "R"),
    ("R", 2, 0, "L"), ("R", 1, 1, "L"), ("F", 3), ("R", 2, 1, "R"), ("R", 2, 1, "L"), ("R", 1, 2, "R"),
    ("R", 1, 2, "L"), ("R", 3, 0, "R"), ("R", 3, 0, "L"), ("R", 2, 2, "R"), ("R", 2, 2, "L"), ("R", 3, 1, "R"),
    ("R", 3, 1, "L"), ("W", 3), ("R", 2, 3, "R"), ("R", 2, 3, "L"), ("R", 3, 2, "R"), ("R", 3, 2, "L"), ("W", 4),
    ("R", 1, 3, "L"), ("R", 1, 3, "R"), ("H", 2), ("R", 3, 3, "R"), ("R", 3, 3, "L"), ("W", 2), ("R", 0, 3, "L"),
    ("R", 0, 3, "R"), ("H", 1), ("H", 3), ("W", 1), ("W", 0), ("H", 0), ("FIN",),
)


def gelu_both(pre_value, grad_value):
    square = pre_value * pre_value
    tanh_part = jnp.tanh(0.7978845608 * (pre_value + 0.044715 * square * pre_value))
    inner_slope = 0.7978845608 * (1.0 + 0.134145 * square)
    value = 0.5 * pre_value * (1.0 + tanh_part)
    slope = 0.5 * (1.0 + tanh_part) + 0.5 * pre_value * (1.0 - tanh_part * tanh_part) * inner_slope
    return value, grad_value * slope


def rows_of(place, count=1):
    return pl.ds(place * 16, count * 16)


def times(left, right):
    return jnp.dot(left, right, preferred_element_type=F32)


def times_transposed(left, right):
    return lax.dot_general(left, right, (((1,), (1,)), ((), ())), preferred_element_type=F32)


def kernel(
    tokens, weight_in, weight_out, grad_out,
    layer_out, grad_tokens, grad_weight_in, grad_weight_out,
    TK, X, WI, WO, PS, PR, YS, YR, HC, HT, GT, SS, SR, OP, ZS, ZR, FS, FR, FO, OB, GI, GO,
    local_sem, a_send, a_recv, j_send, j_recv, c_send, c_recv, z_send, z_recv,
    p_send, p_recv, y_send, y_recv, h_send, h_recv, s_send, s_recv, r_send, r_recv, f_send, f_recv,
):
    dp = lax.axis_index("dp")
    row = lax.axis_index("row")
    z = lax.axis_index("col")
    y, core = dp // 2, dp % 2
    half, x = row // 4, row % 4

    def device(y=y, core=core, half=half, x=x, z=z):
        return {"dp": y * 2 + core, "row": half * 4 + x, "col": z}

    sibling = device(core=1 - core)
    ring = {"R": device(z=(z + 1) % 8), "L": device(z=(z + 7) % 8)}
    across = device(half=1 - half)
    y_peer = {1: device(y=y + 1 - 2 * (y % 2)), 2: device(y=(y + 2) % 4), 3: device(y=3 - y)}
    x_at = {m: (x + m) % 4 for m in (1, 2, 3)}
    x_peer = {m: device(x=x_at[m]) for m in (1, 2, 3)}

    waited = set()

    def send(src, dst, sems, index, to):
        copy = pltpu.make_async_remote_copy(
            src_ref=src, dst_ref=dst, send_sem=sems[0], recv_sem=sems[1].at[index],
            device_id=to, device_id_type=MESH,
        )
        copy.start()

    def arrived(dst, sems, index):
        if (id(sems), index) in waited:
            return
        waited.add((id(sems), index))
        pltpu.make_async_remote_copy(
            src_ref=dst, dst_ref=dst, send_sem=sems[0], recv_sem=sems[1].at[index],
            device_id=sibling, device_id_type=MESH,
        ).wait_recv()

    def all_left(ref, sems):
        pltpu.make_async_remote_copy(
            src_ref=ref, dst_ref=ref, send_sem=sems[0], recv_sem=sems[1].at[0],
            device_id=sibling, device_id_type=MESH,
        ).wait_send()

    a_sem, j_sem, c_sem, z_sem = (a_send, a_recv), (j_send, j_recv), (c_send, c_recv), (z_send, z_recv)
    p_sem, y_sem, h_sem, s_sem = (p_send, p_recv), (y_send, y_recv), (h_send, h_recv), (s_send, s_recv)
    r_sem, f_sem = (r_send, r_recv), (f_send, f_recv)

    barrier = pltpu.get_barrier_semaphore()
    peers = [sibling, *ring.values(), *y_peer.values(), *x_peer.values()]
    peers += [across]
    for peer in peers:
        pl.semaphore_signal(barrier, inc=1, device_id=peer, device_id_type=MESH)
    fetch = [
        pltpu.make_async_copy(tokens, TK.at[0], local_sem.at[0]),
        pltpu.make_async_copy(grad_out, TK.at[1], local_sem.at[1]),
        pltpu.make_async_copy(weight_in, WI, local_sem.at[2]),
        pltpu.make_async_copy(weight_out, WO, local_sem.at[3]),
    ]
    for copy in fetch:
        copy.start()

    pl.semaphore_wait(barrier, len(peers))
    fetch[0].wait()
    fetch[1].wait()

    def fill(distances):
        for r in distances:
            for a in range(2):
                X[0, a, rows_of(PLACE[r])] = TK[a, (z + r) % 8]

    def do_a():
        fill((0, 4))
        for j in (1, 2, 3):
            send(X.at[0, :, rows_of(0, 2)], X.at[j, :, rows_of(0, 2)], a_sem, j - 1, y_peer[j])

    def do_j():
        fill((1, 2, 3, 5, 6, 7))
        send(X.at[0, :, 0:128], X.at[0, :, 128:256], j_sem, 0, sibling)

    def z_rows(s, d):
        return rows_of(2 if d == "R" else 4, 2) if s == 0 else rows_of(7 if d == "R" else 6)

    def z_arrived(j, s, d):
        arrived(X.at[j, :, z_rows(s, d)], z_sem, ((j - 1) * 2 + s) * 2 + "RL".index(d))

    def do_z(j, s, d):
        if s == 0:
            arrived(X.at[j, :, rows_of(0, 2)], a_sem, j - 1)
            source = rows_of(0, 2)
        else:
            z_arrived(j, 0, d)
            source = rows_of(2 if d == "R" else 4)
        index = ((j - 1) * 2 + s) * 2 + "RL".index(d)
        send(X.at[j, :, source], X.at[j, :, z_rows(s, d)], z_sem, index, ring[d])

    def do_s(j, part):
        if part == 0:
            arrived(X.at[j, :, rows_of(0, 2)], a_sem, j - 1)
        for d in "RL":
            z_arrived(j, part, d)
        q, n = ((0, 6), (6, 2))[part]
        send(X.at[j, :, rows_of(q, n)], X.at[j, :, rows_of(8 + q, n)], c_sem, j - 1, sibling)

    def do_c(j):
        if j == 0:
            arrived(X.at[0, :, 128:256], j_sem, 0)
        else:
            arrived(X.at[j, :, 128:256], c_sem, j - 1)
        PS[:, j, 0] = times(X[j, 0], WI[...]).astype(BF16).reshape(4, 64, 384)
        PS[:, j, 1] = times_transposed(X[j, 1], WO[...]).astype(BF16).reshape(4, 64, 384)
        for m in (2, 1, 3):
            send(PS.at[x_at[m], j], PR.at[m - 1, j], p_sem, j, x_peer[m])

    def do_d(j):
        arrived(PR.at[:, j], p_sem, j)
        total = PS[x, j].astype(F32)
        for m in (1, 2, 3):
            total = total + PR[m - 1, j].astype(F32)
        YS[j] = total.astype(BF16)
        send(YS.at[j], YR.at[j], y_sem, j, across)

    def do_e(j):
        arrived(YR.at[j], y_sem, j)
        pre, grad = (YS[j, a].astype(F32) + YR[j, a].astype(F32) for a in (0, 1))
        value, slope = gelu_both(pre, grad)
        HC[j, 0, x] = value.astype(BF16)
        HC[j, 1, x] = slope.astype(BF16)
        for m in (2, 1, 3):
            send(HC.at[j, :, x], HC.at[j, :, x], h_sem, j, x_peer[m])

    def do_f(j):
        arrived(PR.at[:, j], h_sem, j)
        for a in (0, 1):
            lhs = HC[j, a].reshape(256, 384)
            val = times(lhs, WO[...]) if a == 0 else times_transposed(lhs, WI[...])
            OP[j, a] = val[0:128]
            SS[j, a] = val[128:256].astype(BF16)
            send(SS.at[j, a], SR.at[j, a], s_sem, j * 2 + a, sibling)
        HT[:, j * 256:(j + 1) * 256] = HC[j, 0].reshape(256, 384).T
        GT[:, j * 256:(j + 1) * 256] = HC[j, 1].reshape(256, 384).T

    def r_index(j, i, d):
        return (j * 4 + i) * 2 + "RL".index(d)

    def r_ref(buffer, j, i, d):
        direction = "RL".index(d)
        if i == 0:
            return buffer.at[j, i, direction, direction]
        return buffer.at[j, i, direction]

    def both_cores(j, r, a):
        rows = rows_of(PLACE[r])
        return OP[j, a, rows] + SR[j, a, rows].astype(F32)

    def received(j, i, d, a):
        return ZR[j, i, "RL".index(d), a].astype(F32)

    def do_r(j, i, d):
        direction = "RL".index(d)
        for a in (0, 1) if i else (direction,):
            arrived(SR.at[j, a], s_sem, j * 2 + a)
        r = 4 - i if d == "R" else 4 + i
        if i:
            arrived(r_ref(ZR, j, i - 1, d), r_sem, r_index(j, i - 1, d))
        for a in (0, 1) if i else (direction,):
            total = both_cores(j, r, a)
            if i > 1 or (i == 1 and a == direction):
                total = total + received(j, i - 1, d, a)
            ZS[j, i, direction, a] = total.astype(BF16)
        send(r_ref(ZS, j, i, d), r_ref(ZR, j, i, d), r_sem, r_index(j, i, d), ring[d])

    def do_h(j):
        for a in (0, 1):
            arrived(SR.at[j, a], s_sem, j * 2 + a)
        for d in "RL":
            arrived(r_ref(ZR, j, 3, d), r_sem, r_index(j, 3, d))
        for a in (0, 1):
            total = both_cores(j, 0, a) + received(j, 3, "R", a) + received(j, 3, "L", a)
            if j == 0:
                FO[a] = total
            else:
                FS[j - 1, a] = total.astype(BF16)
        if j:
            send(FS.at[j - 1], FR.at[j - 1], f_sem, j - 1, y_peer[j])

    def do_w(k):
        cols = pl.ds(k * 256, min(256, 1152 - k * 256))
        GI[cols, :] = times(GT[...], X[:, 0, :, cols].reshape(1024, cols.size)).T.astype(BF16)
        GO[:, cols] = times(HT[...], X[:, 1, :, cols].reshape(1024, cols.size)).astype(BF16)

    def do_fin():
        stores = [
            pltpu.make_async_copy(GI, grad_weight_in, local_sem.at[4]),
            pltpu.make_async_copy(GO, grad_weight_out, local_sem.at[5]),
        ]
        for copy in stores:
            copy.start()
        total = FO[...]
        for j in (1, 2, 3):
            arrived(FR.at[j - 1], f_sem, j - 1)
            total = total + FR[j - 1].astype(F32)
        OB[...] = total.astype(BF16)
        stores.append(pltpu.make_async_copy(OB.at[0], layer_out, local_sem.at[6]))
        stores.append(pltpu.make_async_copy(OB.at[1], grad_tokens, local_sem.at[7]))
        stores[2].start()
        stores[3].start()
        all_left(X.at[1:4, :, 0:32], a_sem)
        all_left(X.at[0, :, 0:128], j_sem)
        all_left(X.at[1:4, :, 0:128], c_sem)
        all_left(X.at[1:4, :, 0:96], z_sem)
        all_left(PR, p_sem)
        all_left(YS, y_sem)
        all_left(PR, h_sem)
        all_left(SS, s_sem)
        all_left(X.at[:, :, 0:112], r_sem)
        all_left(FS, f_sem)
        for copy in stores:
            copy.wait()

    steps = {
        "A": do_a, "J": do_j, "Z": do_z, "S": do_s, "C": do_c, "D": do_d, "E": do_e, "F": do_f,
        "R": do_r, "H": do_h, "W": do_w, "FIN": do_fin,
    }
    weights_here = False
    for step in ORDER:
        if step[0] == "C" and not weights_here:
            fetch[2].wait()
            fetch[3].wait()
            weights_here = True
        steps[step[0]](*step[1:])


def hand_out(*refs):
    results, outputs, held, arrive, leave = refs[0:4], refs[4:8], refs[8:12], refs[12], refs[13]
    parts = [(i, pl.ds(half * rows, rows)) for half in (0, 1) for i, rows in ((2, 576), (3, 192))]
    parts += [(i, pl.ds(0, 16)) for i in (0, 1)]
    fetches = [pltpu.make_async_copy(results[i].at[p], held[i].at[p], arrive.at[n]) for n, (i, p) in enumerate(parts)]
    stores = [pltpu.make_async_copy(held[i].at[p], outputs[i].at[p], leave.at[n]) for n, (i, p) in enumerate(parts)]
    for fetch in fetches:
        fetch.start()
    for fetch, store in zip(fetches, stores):
        fetch.wait()
        store.start()
    for store in stores:
        store.wait()


def shards(tokens, weight_in, weight_out, grad_out):
    any_space = pl.BlockSpec(memory_space=pl.ANY)
    dma = pltpu.SemaphoreType.DMA
    shapes = (
        jax.ShapeDtypeStruct((16, 1152), BF16),
        jax.ShapeDtypeStruct((16, 1152), BF16),
        jax.ShapeDtypeStruct((1152, 384), BF16),
        jax.ShapeDtypeStruct((384, 1152), BF16),
    )
    results = pl.pallas_call(
        kernel,
        out_shape=shapes,
        in_specs=[any_space] * 4,
        out_specs=(any_space,) * 4,
        scratch_shapes=[
            pltpu.VMEM((2, 8, 16, 1152), BF16),
            pltpu.VMEM((4, 2, 256, 1152), BF16),
            pltpu.VMEM((1152, 384), BF16),
            pltpu.VMEM((384, 1152), BF16),
            pltpu.VMEM((4, 4, 2, 64, 384), BF16),
            pltpu.VMEM((3, 4, 2, 64, 384), BF16),
            pltpu.VMEM((4, 2, 64, 384), BF16),
            pltpu.VMEM((4, 2, 64, 384), BF16),
            pltpu.VMEM((4, 2, 4, 64, 384), BF16),
            pltpu.VMEM((384, 1024), BF16),
            pltpu.VMEM((384, 1024), BF16),
            pltpu.VMEM((4, 2, 128, 1152), BF16),
            pltpu.VMEM((4, 2, 128, 1152), BF16),
            pltpu.VMEM((4, 2, 128, 1152), F32),
            pltpu.VMEM((4, 4, 2, 2, 16, 1152), BF16),
            pltpu.VMEM((4, 4, 2, 2, 16, 1152), BF16),
            pltpu.VMEM((3, 2, 16, 1152), BF16),
            pltpu.VMEM((3, 2, 16, 1152), BF16),
            pltpu.VMEM((2, 16, 1152), F32),
            pltpu.VMEM((2, 16, 1152), BF16),
            pltpu.VMEM((1152, 384), BF16),
            pltpu.VMEM((384, 1152), BF16),
            dma((8,)),
            dma, dma((3,)),
            dma, dma((1,)),
            dma, dma((3,)),
            dma, dma((12,)),
            dma, dma((4,)),
            dma, dma((4,)),
            dma, dma((4,)),
            dma, dma((8,)),
            dma, dma((32,)),
            dma, dma((3,)),
        ],
        compiler_params=pltpu.CompilerParams(
            collective_id=0, has_side_effects=True, vmem_limit_bytes=56 * 1024 * 1024
        ),
        cost_estimate=pl.CostEstimate(flops=5436000000, bytes_accessed=8000000, transcendentals=1000000),
    )(tokens.reshape(8, 16, 1152), weight_in, weight_out, grad_out.reshape(8, 16, 1152))
    return pl.pallas_call(
        hand_out,
        out_shape=shapes,
        in_specs=[any_space] * 4,
        out_specs=(any_space,) * 4,
        scratch_shapes=[*(pltpu.VMEM(shape.shape, BF16) for shape in shapes), dma((6,)), dma((6,))],
    )(*results)


def solution(mesh):
    placed = (P("dp", "row"), P("row", ("dp", "col")), P(("dp", "col"), "row"), P("dp", "row"))
    return jax.shard_map(
        shards,
        mesh=mesh,
        in_specs=placed,
        out_specs=(
            P(("dp", "col"), "row"),
            P(("dp", "col"), "row"),
            P("row", ("dp", "col")),
            P(("dp", "col"), "row"),
        ),
        check_vma=False,
    )
```
